32 devices in a mesh: dp: 8 (over y, x, core), tsp: 4 (over z).
Axes of the slice: x: 2, y: 2, z: 4, core: 2. Of those that a mesh axis runs over, the one named last changes fastest.
Arguments:
- tokens: bfloat16 [16384, 8192], P('dp', 'tsp'), may hold values from -6 to 6
- cotangent: bfloat16 [16384, 1024], P('dp', 'tsp'), may hold values from -6 to 6
- frozen_key_weight: bfloat16 [8192, 1024], P('tsp'), may hold values from -0.1875 to 0.1875
- adapter_down_weight: bfloat16 [16, 64, 8192], P('dp', None, 'tsp'), may hold values from -0.0625 to 0.0625
- adapter_up_weight: bfloat16 [16, 64, 1024], P('dp', None, 'tsp'), may hold values from -0.1875 to 0.1875
- adapter_place_table: int32 [16], replicated, may hold values from 0 to 15, as said below
- segment_adapter: int32 [128], P('dp'), may hold values from 0 to 15, as said below
- segment_live_count: int32 [128], P('dp'), may hold values from 1 to 128, as said below
Outputs:
- token_gradient: bfloat16 [16384, 8192], P('dp', 'tsp')
- down_grad: float32 [16, 64, 8192], P('dp', None, 'tsp')
- up_grad: float32 [16, 64, 1024], P('dp', None, 'tsp')
The draws below stay inside these ranges and needn't reach their ends.
Inputs may be any that keep to these rules, and one draw needn't show every extreme that they name: A permutation: adapter a is held at place adapter_place_table[a], that is by the dp index adapter_place_table[a] // 2 as its entry adapter_place_table[a] % 2; the adapters' arrays and gradients are indexed by place. `segment_adapter`: the 16 segments of one dp index name at most one adapter held by any one dp index; an adapter may be named by several of them. `segment_live_count`: the live rows stand at the start of each segment; on every dp index some segment is full.
All inputs are finite; a program needn't handle non-finite values.
Results may differ from the reference program's by a relative error of at most 0.0034.
Values may be sent and summed in bfloat16 or wider, within the bound.
No kernel may reach another device: no remote copies, remote signals or barrier semaphores. Data moves between devices by JAX's collectives and lax.ppermute only.
A program may use at most 128 MiB of HBM per device.

```python
import jax
import jax.numpy as jnp
from jax import lax

MODEL_WIDTH = 8192
KEY_WIDTH = 1024
ADAPTER_RANKS = 64
SEGMENT_ROWS = 128
ADAPT_DEV = 2
SEG_DEV = 16
ADAPTER_TOTAL = 16
TOKENS = 16384
N_DP = 8


def storage_order(key):
    return jax.random.permutation(jax.random.fold_in(key, 11), ADAPTER_TOTAL).astype(jnp.int32)


def draw_adapter_place_table(key, part):
    return storage_order(key)


def draw_segment_adapter(key, part):
    order = storage_order(key)
    inverse = jnp.argsort(order, stable=True).astype(jnp.int32)
    distinct = min(N_DP, SEG_DEV - SEG_DEV // 8)
    scores = jax.random.randint(jax.random.fold_in(key, 21), (N_DP, N_DP), 0, 1 << 20) * N_DP + jnp.arange(N_DP, dtype=jnp.int32)[None, :]
    owners = jnp.argsort(scores, axis=1, stable=True)[:, :distinct].astype(jnp.int32)
    entries = jax.random.randint(jax.random.fold_in(key, 22), (N_DP, distinct), 0, ADAPT_DEV)
    chosen = owners * ADAPT_DEV + entries
    extra = jax.random.randint(jax.random.fold_in(key, 23), (N_DP, SEG_DEV - distinct), 0, distinct)
    firsts = jnp.broadcast_to(jnp.arange(distinct, dtype=jnp.int32)[None, :], (N_DP, distinct))
    picks = jnp.concatenate([firsts, extra.astype(jnp.int32)], axis=1)
    positions = jnp.take_along_axis(chosen, picks, axis=1)
    shuffle = jax.random.randint(jax.random.fold_in(key, 24), (N_DP, SEG_DEV), 0, 1 << 20) * SEG_DEV + jnp.arange(SEG_DEV, dtype=jnp.int32)[None, :]
    reorder = jnp.argsort(shuffle, axis=1, stable=True)
    positions = jnp.take_along_axis(positions, reorder, axis=1)
    return inverse[positions.reshape(-1)].astype(jnp.int32)


def draw_segment_live_count(key, part):
    counts = jax.random.randint(jax.random.fold_in(key, 31), (N_DP, SEG_DEV), 1, SEGMENT_ROWS + 1)
    full_at = jax.random.randint(jax.random.fold_in(key, 32), (N_DP, 1), 0, SEG_DEV)
    counts = jnp.where(jnp.arange(SEG_DEV, dtype=jnp.int32)[None, :] == full_at, SEGMENT_ROWS, counts)
    return counts.reshape(-1).astype(jnp.int32)


def levels(stream_key, shape, shards, smallest, high):
    factor_of = 1.0
    for dim, shards_of in shards:
        heights = jax.random.uniform(jax.random.fold_in(jax.random.fold_in(stream_key, 6), dim), (shards_of,), jnp.float32, smallest / len(shards), high / len(shards))
        factor_of = factor_of * jnp.repeat(jnp.exp(heights), shape[dim] // shards_of).reshape((-1,) + (1,) * (len(shape) - 1 - dim))
    return factor_of


def centred(stream_key, dims, spread, most, pieces=(), kind=jnp.bfloat16):
    result = jax.random.normal(stream_key, dims, jnp.float32) * spread
    if len(pieces) > 0:
        result = levels(stream_key, dims, pieces, -0.22, 0.18) * result
    return jnp.clip(result, min=-most, max=most).astype(kind)


def setup_inputs(seed: int = 0) -> dict:
    key_list = jax.random.split(jax.random.key(seed), 9)
    tokens = centred(key_list[0], (TOKENS, MODEL_WIDTH), 1.0, 6.0, ((0, 8), (1, 4)))
    cotangent = centred(key_list[1], (TOKENS, KEY_WIDTH), 1.0, 6.0, ((0, 8), (1, 4)))
    frozen_key_weight = centred(key_list[2], (MODEL_WIDTH, KEY_WIDTH), KEY_WIDTH ** -0.5, 0.1875, ((0, 4),))
    adapter_down_weight = centred(key_list[3], (ADAPTER_TOTAL, ADAPTER_RANKS, MODEL_WIDTH), MODEL_WIDTH ** -0.5, 0.0625, ((0, 8), (2, 4)))
    adapter_up_weight = centred(key_list[4], (ADAPTER_TOTAL, ADAPTER_RANKS, KEY_WIDTH), KEY_WIDTH ** -0.5, 0.1875, ((0, 8), (2, 4)))
    adapter_place_table = draw_adapter_place_table(jax.random.fold_in(key_list[8], 71), 0)
    segment_adapter = draw_segment_adapter(jax.random.fold_in(key_list[8], 71), 0)
    segment_live_count = draw_segment_live_count(jax.random.fold_in(key_list[8], 71), 0)
    return dict(tokens=tokens, cotangent=cotangent, frozen_key_weight=frozen_key_weight, adapter_down_weight=adapter_down_weight, adapter_up_weight=adapter_up_weight, adapter_place_table=adapter_place_table, segment_adapter=segment_adapter, segment_live_count=segment_live_count)


ADAPTER_SCALE = 2.0


def reference(tokens, cotangent, frozen_key_weight, adapter_down_weight, adapter_up_weight, adapter_place_table, segment_adapter, segment_live_count):
    tok_block = SEGMENT_ROWS * SEG_DEV

    def one_block(carry, block):
        down_total, up_total = carry
        first = (block * tok_block).astype(jnp.int32)
        rows_x = lax.dynamic_slice_in_dim(tokens, first, tok_block, 0)
        rows_dy = lax.dynamic_slice_in_dim(cotangent, first, tok_block, 0)
        seg_first = (block * SEG_DEV).astype(jnp.int32)
        idents = lax.dynamic_slice_in_dim(segment_adapter, seg_first, SEG_DEV, 0)
        counts = lax.dynamic_slice_in_dim(segment_live_count, seg_first, SEG_DEV, 0)
        adapter_places = adapter_place_table[idents].astype(jnp.int32)
        segment_down_weight = adapter_down_weight[adapter_places].astype(jnp.float32)
        segment_up_weight = adapter_up_weight[adapter_places].astype(jnp.float32)
        live_mask = (jnp.arange(SEGMENT_ROWS, dtype=jnp.int32)[None, :] < counts[:, None]).astype(jnp.float32)
        input_rows = rows_x.reshape(SEG_DEV, SEGMENT_ROWS, MODEL_WIDTH).astype(jnp.float32)
        incoming_gradient = rows_dy.reshape(SEG_DEV, SEGMENT_ROWS, KEY_WIDTH).astype(jnp.float32)
        reduced_rows = (jnp.einsum("gtd,grd->gtr", input_rows, segment_down_weight) * live_mask[:, :, None]).astype(jnp.bfloat16)
        gathered_weights = (jnp.einsum("gtk,grk->gtr", incoming_gradient, segment_up_weight) * live_mask[:, :, None]).astype(jnp.bfloat16)
        frozen_output = jnp.dot(rows_dy, frozen_key_weight.T, preferred_element_type=jnp.float32).reshape(SEG_DEV, SEGMENT_ROWS, MODEL_WIDTH)
        adapter_output = jnp.einsum("wks,wsx->wkx", gathered_weights.astype(jnp.float32), segment_down_weight)
        token_gradient = ((frozen_output + ADAPTER_SCALE * adapter_output) * live_mask[:, :, None]).astype(jnp.bfloat16)
        segment_down_gradient = jnp.einsum("upf,upb->ufb", gathered_weights.astype(jnp.float32), input_rows) * (ADAPTER_SCALE / SEGMENT_ROWS)
        segment_up_gradient = jnp.einsum("ija,ijn->ian", reduced_rows.astype(jnp.float32), incoming_gradient) * (ADAPTER_SCALE / SEGMENT_ROWS)
        down_total = down_total.at[adapter_places].add(segment_down_gradient)
        up_total = up_total.at[adapter_places].add(segment_up_gradient)
        return (down_total, up_total), token_gradient.reshape(tok_block, MODEL_WIDTH)

    start = (jnp.zeros((ADAPTER_TOTAL, ADAPTER_RANKS, MODEL_WIDTH), jnp.float32), jnp.zeros((ADAPTER_TOTAL, ADAPTER_RANKS, KEY_WIDTH), jnp.float32))
    (down_grad, up_grad), blocks = lax.scan(one_block, start, jnp.arange(N_DP, dtype=jnp.int32))
    return blocks.reshape(TOKENS, MODEL_WIDTH), down_grad, up_grad
```

```python
import functools

import jax
import jax.numpy as jnp
from jax import lax
from jax.experimental import pallas as pl
from jax.experimental.pallas import tpu as pltpu
from jax.sharding import PartitionSpec as P

ADAPTER_SCALE = 2.0
ANY = pl.BlockSpec(memory_space=pl.ANY)
SMEM = pl.BlockSpec(memory_space=pltpu.SMEM)
VMEM = pl.BlockSpec(memory_space=pltpu.VMEM)
NT = (((1,), (1,)), ((), ()))
TN = (((0,), (0,)), ((), ()))
NN = (((1,), (0,)), ((), ()))
LIMIT = 56 * 1024 * 1024


def lookup(idents, mapping):
    matches = idents[:, None] == jnp.arange(mapping.shape[0], dtype=jnp.int32)[None, :]
    return jnp.sum(jnp.where(matches, mapping[None, :], 0), axis=1)


def params():
    return pltpu.CompilerParams(vmem_limit_bytes=LIMIT)


def load_all(pairs, sem):
    copies = [pltpu.make_async_copy(src, dst, sem.at[i]) for i, (src, dst) in enumerate(pairs)]
    for copy in copies:
        copy.start()
    for copy in copies:
        copy.wait()


def load_line(z, n, own, ups, downs, dst, sem):
    def each(act):
        act(pltpu.make_async_copy(own, dst(z), sem.at[0]))
        for s in range(1, n):

            @pl.when(z >= s)
            def _():
                act(pltpu.make_async_copy(ups[s - 1], dst(z - s), sem.at[s]))

            @pl.when(z + s < n)
            def _():
                act(pltpu.make_async_copy(downs[s - 1], dst(z + s), sem.at[n - 1 + s]))

    each(lambda copy: copy.start())
    each(lambda copy: copy.wait())


def live_mask(count, rows, width):
    return lax.broadcasted_iota(jnp.int32, (rows, width), 0) < count


def pack_kernel(segs, rows, packed, off, cot, *refs):
    outs, buf = refs[:-1], refs[-1]
    buf[...] = jnp.zeros_like(buf)
    for g in range(segs):
        start = pl.multiple_of(off[g], 16)
        buf[pl.ds(start, rows), :] = cot[g * rows : (g + 1) * rows, :]
    part = packed // len(outs)
    for c, out in enumerate(outs):
        out[...] = buf[c * part : (c + 1) * part, :]


def pack(cot, off, segs, packed, chunks):
    rows, width = cot.shape[0] // segs, cot.shape[1]
    return pl.pallas_call(
        functools.partial(pack_kernel, segs, rows, packed),
        out_shape=[jax.ShapeDtypeStruct((packed // chunks, width), cot.dtype)] * chunks,
        in_specs=[SMEM, VMEM],
        out_specs=[VMEM] * chunks,
        scratch_shapes=[pltpu.VMEM((packed + rows, width), cot.dtype)],
        compiler_params=params(),
        name="pack",
    )(off, cot)


def project_kernel(n, per, rows, packed, n_maps, z, idx, off, count, x, *refs):
    maps, refs = refs[:n_maps], refs[n_maps:]
    outs, (table, buf, sem) = refs[: 2 * n - 1], refs[2 * n - 1 :]
    step = pl.program_id(0)

    @pl.when(step == 0)
    def _():
        each = maps[0].shape[0]
        load_all([(m, table.at[pl.ds(i * each, each)]) for i, m in enumerate(maps)], sem)
        buf[...] = jnp.zeros_like(buf)

    for i in range(per):
        g = step * per + i
        term = lax.dot_general(
            x[i * rows : (i + 1) * rows, :], table[idx[g]], NT, preferred_element_type=jnp.float32
        )
        term = jnp.where(live_mask(count[g], *term.shape), term, 0.0)
        buf[pl.ds(pl.multiple_of(off[g], 16), rows), :] = term

    @pl.when(step == pl.num_programs(0) - 1)
    def _():
        block = packed // n
        half = block // 2

        def paired(j):
            start = pl.multiple_of(j * block, 16)
            return jnp.concatenate(
                [buf[pl.ds(start, half), :], buf[pl.ds(start + half, half), :]], axis=1
            )

        outs[0][...] = paired(z[0])
        for s in range(1, n):
            outs[s][...] = paired(jnp.minimum(z[0] + s, n - 1))
            outs[n - 1 + s][...] = paired(jnp.maximum(z[0] - s, 0))


def project(z, idx, off, count, x, maps, n, packed, per):
    segs = idx.shape[0]
    rows, width = x.shape[0] // segs, x.shape[1]
    ranks = maps[0].shape[1]
    total = sum(m.shape[0] for m in maps)
    block = jax.ShapeDtypeStruct((packed // n // 2, 2 * ranks), jnp.float32)
    return pl.pallas_call(
        functools.partial(project_kernel, n, per, rows, packed, len(maps)),
        grid=(segs // per,),
        out_shape=[block] * (2 * n - 1),
        in_specs=[SMEM] * 4
        + [pl.BlockSpec((per * rows, width), lambda i: (i, 0))]
        + [ANY] * len(maps),
        out_specs=[pl.BlockSpec(block.shape, lambda i: (0, 0))] * (2 * n - 1),
        scratch_shapes=[
            pltpu.VMEM((total, ranks, width), x.dtype),
            pltpu.VMEM((packed + rows, ranks), jnp.float32),
            pltpu.SemaphoreType.DMA((len(maps),)),
        ],
        compiler_params=params(),
        name="project",
    )(z, idx, off, count, x, *maps)


def unpair(n, raw, buf):
    half, ranks = raw.shape[1], raw.shape[2] // 2
    for j in range(n):
        buf[pl.ds(2 * j * half, half), :] = raw[j][:, :ranks]
        buf[pl.ds((2 * j + 1) * half, half), :] = raw[j][:, ranks:]
    tail = buf.shape[0] - 2 * n * half
    buf[pl.ds(2 * n * half, tail), :] = jnp.zeros((tail, ranks), buf.dtype)


def sums_kernel(n, per, rows, scale, z, slot, off, count, x, *refs):
    line, refs = refs[: 2 * n - 1], refs[2 * n - 1 :]
    outs, (raw, buf, total, sem) = refs[:-4], refs[-4:]
    step = pl.program_id(0)

    @pl.when(step == 0)
    def _():
        load_line(z[0], n, line[0], line[1:n], line[n:], lambda j: raw.at[j], sem)
        unpair(n, raw, buf)
        total[...] = jnp.zeros_like(total)

    for i in range(per):
        g = step * per + i
        terms = buf[pl.ds(pl.multiple_of(off[g], 16), rows), :]
        terms = jnp.where(live_mask(count[g], *terms.shape), terms, jnp.zeros_like(terms))
        total[slot[g]] += lax.dot_general(
            terms, x[i * rows : (i + 1) * rows, :], TN, preferred_element_type=jnp.float32
        )

    @pl.when(step == pl.num_programs(0) - 1)
    def _():
        for k, out in enumerate(outs):
            out[...] = (total[k] * scale).astype(out.dtype)


def sums(z, slot, off, count, x, line, n, slots, packed, per):
    segs = slot.shape[0]
    rows, width = x.shape[0] // segs, x.shape[1]
    half, ranks = line[0].shape[0], line[0].shape[1] // 2
    outs = [jax.ShapeDtypeStruct((ranks, width), jnp.float32 if k == 0 else jnp.bfloat16) for k in range(slots)]
    return pl.pallas_call(
        functools.partial(sums_kernel, n, per, rows, ADAPTER_SCALE / rows),
        grid=(segs // per,),
        out_shape=outs,
        in_specs=[SMEM] * 4
        + [pl.BlockSpec((per * rows, width), lambda i: (i, 0))]
        + [ANY] * (2 * n - 1),
        out_specs=[pl.BlockSpec((ranks, width), lambda i: (0, 0))] * slots,
        scratch_shapes=[
            pltpu.VMEM((n, half, 2 * ranks), jnp.bfloat16),
            pltpu.VMEM((packed + rows, ranks), jnp.bfloat16),
            pltpu.VMEM((slots, ranks, width), jnp.float32),
            pltpu.SemaphoreType.DMA((2 * n - 1,)),
        ],
        compiler_params=params(),
        name="sums",
    )(z, slot, off, count, x, *line)


def token_kernel(n, per, rows, packed, chunks, n_maps, z, idx, off, count, weight, *refs):
    line = 2 * n - 1
    maps, refs = refs[:n_maps], refs[n_maps:]
    pulled, refs = refs[:line], refs[line:]
    cots, refs = refs[: chunks * line], refs[chunks * line :]
    out, table, raw, ranks_buf, cot, map_sem, line_sem = refs
    part = packed // chunks
    step = pl.program_id(0)

    @pl.when(step == 0)
    def _():
        each = maps[0].shape[0]
        load_all([(m, table.at[pl.ds(i * each, each)]) for i, m in enumerate(maps)], map_sem)
        load_line(z[0], n, pulled[0], pulled[1:n], pulled[n:], lambda j: raw.at[j], line_sem)
        for c in range(chunks):
            got = cots[c * line : (c + 1) * line]
            load_line(
                z[0], n, got[0], got[1:n], got[n:], lambda j: cot.at[j, pl.ds(c * part, part)], line_sem
            )
        cot[:, pl.ds(packed, rows), :] = jnp.zeros((n, rows, cot.shape[2]), cot.dtype)
        unpair(n, raw, ranks_buf)

    key = cot.shape[2]
    width = weight.shape[0]
    tile = min(512, width)
    starts = [pl.multiple_of(off[step * per + i], 16) for i in range(per)]
    counts = [count[step * per + i] for i in range(per)]
    shards = [
        jnp.concatenate([cot[j, pl.ds(start, rows), :] for start in starts], axis=0) for j in range(n)
    ]
    for d in range(0, width, tile):
        total = lax.dot_general(
            shards[0], weight[d : d + tile, :key], NT, preferred_element_type=jnp.float32
        )
        for j in range(1, n):
            total += lax.dot_general(
                shards[j],
                weight[d : d + tile, j * key : (j + 1) * key],
                NT,
                preferred_element_type=jnp.float32,
            )
        for i in range(per):
            terms = ranks_buf[pl.ds(starts[i], rows), :]
            adapter = lax.dot_general(
                terms, table[idx[step * per + i], :, d : d + tile], NN, preferred_element_type=jnp.float32
            )
            both = total[i * rows : (i + 1) * rows, :] + ADAPTER_SCALE * adapter
            both = jnp.where(live_mask(counts[i], rows, tile), both, 0.0)
            out[i * rows : (i + 1) * rows, d : d + tile] = both.astype(out.dtype)


def token_gradients(z, idx, off, count, weight, maps, pulled, cots, n, packed, rows, per):
    segs = idx.shape[0]
    width = weight.shape[0]
    chunks = len(cots)
    key = cots[0][0].shape[1]
    ranks = maps[0].shape[1]
    total = sum(m.shape[0] for m in maps)
    half = pulled[0].shape[0]
    return pl.pallas_call(
        functools.partial(token_kernel, n, per, rows, packed, chunks, len(maps)),
        grid=(segs // per,),
        out_shape=jax.ShapeDtypeStruct((segs * rows, width), jnp.bfloat16),
        in_specs=[SMEM] * 4
        + [pl.BlockSpec(weight.shape, lambda i: (0, 0), pipeline_mode=pl.Buffered(1))]
        + [ANY] * (len(maps) + (chunks + 1) * (2 * n - 1)),
        out_specs=pl.BlockSpec((per * rows, width), lambda i: (i, 0)),
        scratch_shapes=[
            pltpu.VMEM((total, ranks, width), jnp.bfloat16),
            pltpu.VMEM((n, half, 2 * ranks), jnp.bfloat16),
            pltpu.VMEM((packed + rows, ranks), jnp.bfloat16),
            pltpu.VMEM((n, packed + rows, key), jnp.bfloat16),
            pltpu.SemaphoreType.DMA((len(maps),)),
            pltpu.SemaphoreType.DMA((2 * n - 1,)),
        ],
        compiler_params=params(),
        name="token_gradient",
    )(z, idx, off, count, weight, *maps, *pulled, *[a for got in cots for a in got])


def shift(x, n, by):
    return lax.ppermute(x, "tsp", [(i, i + by) for i in range(n) if 0 <= i + by < n])


def gather_line(x, n):
    ups, downs = [x], [x]
    for _ in range(n - 1):
        ups.append(shift(ups[-1], n, 1))
        downs.append(shift(downs[-1], n, -1))
    return [x] + ups[1:] + downs[1:]


def gather_direct(x, n):
    return [x] + [shift(x, n, s) for s in range(1, n)] + [shift(x, n, -s) for s in range(1, n)]


def reduce_blocks(blocks, n):
    total = blocks[0]
    for s in range(1, n):
        total = total + shift(blocks[s], n, s) + shift(blocks[n - 1 + s], n, -s)
    return total.astype(jnp.bfloat16)


def flip(x, n, by):
    return lax.ppermute(x, "dp", [(i, i ^ by) for i in range(n)])


def gather_maps_small(maps, n):
    same = [maps] + [flip(maps, n, k) for k in (2, 4, 6)]
    other = [flip(m, n, 1) for m in same]
    return [m for pair in zip(same, other) for m in pair]


def gather_maps(maps, n):
    half = maps.shape[0] // 2
    low, high = maps[:half], maps[half:]
    over_x, over_y = [flip(m, n, 2) for m in (low, high)], [flip(m, n, 4) for m in (low, high)]
    corner = [flip(over_x[0], n, 4), flip(over_y[1], n, 2)]
    same = [[low, high], over_x, over_y, corner]
    other = [[flip(m, n, 1) for m in pair] for pair in same]
    return [m for a, b in zip(same, other) for m in a + b]


def on_device(
    tokens,
    cotangent,
    frozen_key_weight,
    adapter_down_weight,
    adapter_up_weight,
    adapter_place_table,
    segment_adapter,
    segment_live_count,
):
    n_dp = lax.axis_size("dp")
    n = lax.axis_size("tsp")
    me = lax.axis_index("dp").astype(jnp.int32)
    z = lax.axis_index("tsp").astype(jnp.int32)[None]
    held = adapter_down_weight.shape[0]
    segs = segment_adapter.shape[0]
    rows = tokens.shape[0] // segs
    packed = segs * rows
    cube = n_dp == 8 and held % 2 == 0

    places = lookup(segment_adapter, adapter_place_table)
    owner, entry = places // held, places % held
    peers = jnp.arange(n_dp, dtype=jnp.int32)
    wanted = jnp.max(jnp.where(owner[:, None] == peers[None, :], entry[:, None], -1), axis=0)
    asked = lax.all_gather(wanted, "dp", axis=0, tiled=False)[:, me]
    slot = owner ^ me
    if cube:
        idx = slot * held + entry
        ups = gather_maps_small(adapter_up_weight, n_dp)
        downs = gather_maps(adapter_down_weight, n_dp)
    else:
        idx = places
        ups = [lax.all_gather(adapter_up_weight, "dp", axis=0, tiled=True)]
        downs = [lax.all_gather(adapter_down_weight, "dp", axis=0, tiled=True)]
    count = segment_live_count
    padded = (count + 15) // 16 * 16
    off = jnp.cumsum(padded) - padded

    chunks = pack(cotangent, off, segs, packed, 2)
    cots = [gather_line(chunk, n) for chunk in chunks]

    pulled = reduce_blocks(project(z, idx, off, count, cotangent, ups, n, packed, segs), n)
    pulled = gather_direct(pulled, n)
    lowered = reduce_blocks(project(z, idx, off, count, tokens, downs, n, packed, 2), n)
    lowered = gather_direct(lowered, n)

    token_gradient = token_gradients(
        z, idx, off, count, frozen_key_weight, downs, pulled, cots, n, packed, rows, 2
    )

    def owned(terms, x, per):
        sent = sums(z, slot, off, count, x, terms, n, n_dp, packed, per)
        if n_dp == 8:
            got = [sent[0]] + [flip(sent[k], n_dp, k) for k in range(1, n_dp)]
        else:
            others = jnp.stack([sent[0].astype(jnp.bfloat16)] + list(sent[1:]))
            others = others[peers ^ me]
            others = lax.all_to_all(others, "dp", 0, 0, tiled=True)
            got = [others[k] for k in range(n_dp)]
        grads = []
        for e in range(held):
            total = 0.0
            for k, term in enumerate(got):
                hit = asked[(me ^ k) if n_dp == 8 else k] == e
                total = total + jnp.where(hit, term.astype(jnp.float32), 0.0)
            grads.append(total)
        return jnp.stack(grads)

    down_grad = owned(pulled, tokens, 2)
    up_grad = owned(lowered, cotangent, segs)
    return (token_gradient, down_grad, up_grad)


def solution(mesh):
    placed = (
        P("dp", "tsp"),
        P("dp", "tsp"),
        P("tsp", None),
        P("dp", None, "tsp"),
        P("dp", None, "tsp"),
        P(),
        P("dp"),
        P("dp"),
    )
    return jax.shard_map(
        on_device,
        mesh=mesh,
        in_specs=placed,
        out_specs=(P("dp", "tsp"), P("dp", None, "tsp"), P("dp", None, "tsp")),
        check_vma=False,
    )
```

```python
import functools

import jax
import jax.numpy as jnp
from jax import lax
from jax.experimental import pallas as pl
from jax.experimental.pallas import tpu as pltpu
from jax.sharding import PartitionSpec as P

ADAPTER_SCALE = 2.0
ANY = pl.BlockSpec(memory_space=pl.ANY)
SMEM = pl.BlockSpec(memory_space=pltpu.SMEM)
VMEM = pl.BlockSpec(memory_space=pltpu.VMEM)
NT = (((1,), (1,)), ((), ()))
TN = (((0,), (0,)), ((), ()))
NN = (((1,), (0,)), ((), ()))
MIB = 1024 * 1024


def lookup(idents, mapping):
    matches = idents[:, None] == jnp.arange(mapping.shape[0], dtype=jnp.int32)[None, :]
    return jnp.sum(jnp.where(matches, mapping[None, :], 0), axis=1)


def params(mib):
    return pltpu.CompilerParams(vmem_limit_bytes=mib * MIB)


def cost(us):
    return pl.CostEstimate(flops=0, bytes_accessed=int(us * 3e5), transcendentals=0)


def load_all(pairs, sem):
    copies = [pltpu.make_async_copy(src, dst, sem.at[i]) for i, (src, dst) in enumerate(pairs)]
    for copy in copies:
        copy.start()
    for copy in copies:
        copy.wait()


def live_mask(count, rows, width):
    return lax.broadcasted_iota(jnp.int32, (rows, width), 0) < count


def pack_kernel(segs, rows, sizes, off, cot, *refs):
    outs, buf = refs[-1 - len(sizes) : -1], refs[-1]
    buf[...] = jnp.zeros_like(buf)
    for g in range(segs):
        start = pl.multiple_of(off[g], 16)
        buf[pl.ds(start, rows), :] = cot[g * rows : (g + 1) * rows, :]
    first = 0
    for out, size in zip(outs, sizes):
        out[...] = buf[first : first + size, :]
        first += size


def pack(cot, off, segs, sizes, after=()):
    rows, width = cot.shape[0] // segs, cot.shape[1]
    return pl.pallas_call(
        functools.partial(pack_kernel, segs, rows, sizes),
        out_shape=[jax.ShapeDtypeStruct((size, width), cot.dtype) for size in sizes],
        in_specs=[SMEM, VMEM] + [ANY] * len(after),
        out_specs=[VMEM] * len(sizes),
        scratch_shapes=[pltpu.VMEM((segs * rows + rows, width), cot.dtype)],
        compiler_params=params(8),
        cost_estimate=cost(1),
        name="pack",
    )(off, cot, *after)


def project_kernel(n, per, rows, packed, n_maps, idx, off, count, x, *refs):
    maps, (out, table, buf, sem) = refs[:n_maps], refs[-4:]
    step = pl.program_id(0)

    @pl.when(step == 0)
    def _():
        each = maps[0].shape[0]
        load_all([(m, table.at[pl.ds(i * each, each)]) for i, m in enumerate(maps)], sem)
        buf[...] = jnp.zeros_like(buf)

    for i in range(per):
        g = step * per + i
        term = lax.dot_general(
            table[idx[g]], x[i * rows : (i + 1) * rows, :], NT, preferred_element_type=jnp.float32
        ).T
        term = jnp.where(live_mask(count[g], *term.shape), term, 0.0)
        buf[pl.ds(pl.multiple_of(off[g], 16), rows), :] = term

    @pl.when(step == pl.num_programs(0) - 1)
    def _():
        half = packed // n // 2
        for j in range(n):
            start = 2 * j * half
            out[j] = jnp.concatenate(
                [buf[start : start + half, :], buf[start + half : start + 2 * half, :]], axis=1
            )


def project(idx, off, count, x, maps, n, packed, per, us, after=()):
    segs = idx.shape[0]
    rows, width = x.shape[0] // segs, x.shape[1]
    ranks = maps[0].shape[1]
    total = sum(m.shape[0] for m in maps)
    shape = (n, packed // n // 2, 2 * ranks)
    return pl.pallas_call(
        functools.partial(project_kernel, n, per, rows, packed, len(maps)),
        grid=(segs // per,),
        out_shape=jax.ShapeDtypeStruct(shape, jnp.float32),
        in_specs=[SMEM] * 3
        + [pl.BlockSpec((per * rows, width), lambda i: (i, 0))]
        + [ANY] * (len(maps) + len(after)),
        out_specs=pl.BlockSpec(shape, lambda i: (0, 0, 0)),
        scratch_shapes=[
            pltpu.VMEM((total, ranks, width), x.dtype),
            pltpu.VMEM((segs * rows + rows, ranks), jnp.float32),
            pltpu.SemaphoreType.DMA((len(maps),)),
        ],
        compiler_params=params(60),
        cost_estimate=cost(us),
        name="project",
    )(idx, off, count, x, *maps, *after)


def cot_copies(n, z, sizes, cots, cot, sem):
    key = cots[0].shape[1]
    copies, first = [], 0
    for c, size in enumerate(sizes):
        for s in range(n):
            column = pl.multiple_of(lax.rem(z - s + n, n) * key, key)
            dst = cot.at[pl.ds(first, size), pl.ds(column, key)]
            copies.append(pltpu.make_async_copy(cots[c * n + s], dst, sem.at[c * n + s]))
        first += size
    return copies


def add_terms(total, owner, terms, x):
    total[owner] += lax.dot_general(terms, x, TN, preferred_element_type=jnp.float32)


def up_sums_kernel(rows, scale, owner, off, count, x, raw, sent, out, buf, total):
    del sent
    n, half, ranks = raw.shape[0], raw.shape[1], raw.shape[2] // 2
    packed = 2 * n * half
    for j in range(n):
        start = 2 * j * half
        buf[start : start + half, :] = raw[j][:, :ranks]
        buf[start + half : start + 2 * half, :] = raw[j][:, ranks:]
    buf[packed : packed + rows, :] = jnp.zeros((rows, ranks), buf.dtype)
    total[...] = jnp.zeros_like(total)
    for g in range(x.shape[0] // rows):
        terms = buf[pl.ds(pl.multiple_of(off[g], 16), rows), :]
        terms = jnp.where(live_mask(count[g], *terms.shape), terms, jnp.zeros_like(terms))
        add_terms(total, owner[g], terms, x[g * rows : (g + 1) * rows, :])
    out[...] = (total[...] * scale).astype(out.dtype)


def up_sums(owner, off, count, x, lowered, sent, us):
    segs = owner.shape[0]
    rows, width = x.shape[0] // segs, x.shape[1]
    packed, ranks = 2 * lowered.shape[0] * lowered.shape[1], lowered.shape[2] // 2
    owners, last = sent.shape[0], sent.shape[2] // width - 1
    return pl.pallas_call(
        functools.partial(up_sums_kernel, rows, ADAPTER_SCALE / rows),
        grid=(1,),
        out_shape=jax.ShapeDtypeStruct(sent.shape, sent.dtype),
        in_specs=[SMEM] * 3 + [VMEM] * 2 + [ANY],
        out_specs=pl.BlockSpec((owners, ranks, width), lambda i: (0, 0, last)),
        scratch_shapes=[
            pltpu.VMEM((packed + rows, ranks), jnp.bfloat16),
            pltpu.VMEM((owners, ranks, width), jnp.float32),
        ],
        input_output_aliases={5: 0},
        compiler_params=params(12),
        cost_estimate=cost(us),
        name="up_sums",
    )(owner, off, count, x, lowered, sent)


def down_sums_kernel(n, per, rows, sizes, n_maps, scale, z, idx, owner, off, count, x, *refs):
    maps, refs = refs[:n_maps], refs[n_maps:]
    cots, refs = refs[: n * len(sizes)], refs[n * len(sizes) :]
    out, pulled, table, cot, total, map_sem, cot_sem = refs[-7:]
    step = pl.program_id(0)
    packed = sum(sizes)

    @pl.when(step == 0)
    def _():
        copies = cot_copies(n, z[0], sizes, cots, cot, cot_sem)
        parts, held, _, key = maps[0].shape
        for i, m in enumerate(maps):
            for j in range(parts):
                column = pl.multiple_of(lax.rem(z[0] - j + n, n) * key, key)
                dst = table.at[pl.ds(i * held, held), :, pl.ds(column, key)]
                copies.append(pltpu.make_async_copy(m.at[j], dst, map_sem.at[i * parts + j]))
        for copy in copies:
            copy.start()
        total[...] = jnp.zeros_like(total)
        cot[packed : packed + rows, :] = jnp.zeros((rows, cot.shape[1]), cot.dtype)
        for copy in copies:
            copy.wait()

    for i in range(per):
        g = step * per + i
        terms = lax.dot_general(
            cot[pl.ds(pl.multiple_of(off[g], 16), rows), :],
            table[idx[g]],
            NT,
            preferred_element_type=jnp.float32,
        )
        terms = jnp.where(live_mask(count[g], *terms.shape), terms, 0.0).astype(pulled.dtype)
        pulled[i * rows : (i + 1) * rows, :] = terms
        add_terms(total, owner[g], terms, x[i * rows : (i + 1) * rows, :])

    @pl.when(step == pl.num_programs(0) - 1)
    def _():
        out[:, :, : x.shape[1]] = (total[...] * scale).astype(out.dtype)


def down_sums(z, idx, owner, off, count, x, maps, cots, owners, n, per, us, extra):
    segs = owner.shape[0]
    rows, width = x.shape[0] // segs, x.shape[1]
    sizes = [got[0].shape[0] for got in cots]
    parts, held, ranks, key = maps[0].shape
    shape = (owners, ranks, width)
    wide = (owners, ranks, width + extra)
    return pl.pallas_call(
        functools.partial(down_sums_kernel, n, per, rows, sizes, len(maps), ADAPTER_SCALE / rows),
        grid=(segs // per,),
        out_shape=[
            jax.ShapeDtypeStruct(wide, jnp.bfloat16),
            jax.ShapeDtypeStruct((segs * rows, ranks), jnp.bfloat16),
        ],
        in_specs=[SMEM] * 5
        + [pl.BlockSpec((per * rows, width), lambda i: (i, 0))]
        + [ANY] * (len(maps) + n * len(sizes)),
        out_specs=[
            pl.BlockSpec(wide, lambda i: (0, 0, 0)),
            pl.BlockSpec((per * rows, ranks), lambda i: (i, 0)),
        ],
        scratch_shapes=[
            pltpu.VMEM((held * len(maps), ranks, parts * key), jnp.bfloat16),
            pltpu.VMEM((sum(sizes) + rows, n * key), jnp.bfloat16),
            pltpu.VMEM(shape, jnp.float32),
            pltpu.SemaphoreType.DMA((parts * len(maps),)),
            pltpu.SemaphoreType.DMA((n * len(sizes),)),
        ],
        compiler_params=params(60),
        cost_estimate=cost(us),
        name="down_sums",
    )(z, idx, owner, off, count, x, *maps, *[a for got in cots for a in got])


def token_kernel(n, per, rows, sizes, n_maps, z, idx, off, count, weight, pulled, *refs):
    maps, refs = refs[:n_maps], refs[n_maps:]
    cots, (out, table, cot, map_sem, cot_sem) = refs[:-5], refs[-5:]
    packed = sum(sizes)
    step = pl.program_id(0)

    @pl.when(step == 0)
    def _():
        each = maps[0].shape[0]
        copies = cot_copies(n, z[0], sizes, cots, cot, cot_sem)
        for i, m in enumerate(maps):
            copies.append(pltpu.make_async_copy(m, table.at[pl.ds(i * each, each)], map_sem.at[i]))
        for copy in copies:
            copy.start()
        cot[packed : packed + rows, :] = jnp.zeros((rows, cot.shape[1]), cot.dtype)
        for copy in copies:
            copy.wait()

    width = weight.shape[0]
    tile = min(512, width)
    starts = [pl.multiple_of(off[step * per + i], 16) for i in range(per)]
    counts = [count[step * per + i] for i in range(per)]
    x = jnp.concatenate([cot[pl.ds(start, rows), :] for start in starts], axis=0)
    for d in range(0, width, tile):
        total = lax.dot_general(x, weight[d : d + tile, :], NT, preferred_element_type=jnp.float32)
        for i in range(per):
            adapter = lax.dot_general(
                pulled[i * rows : (i + 1) * rows, :],
                table[idx[step * per + i], :, d : d + tile],
                NN,
                preferred_element_type=jnp.float32,
            )
            both = total[i * rows : (i + 1) * rows, :] + ADAPTER_SCALE * adapter
            both = jnp.where(live_mask(counts[i], rows, tile), both, 0.0)
            out[i * rows : (i + 1) * rows, d : d + tile] = both.astype(out.dtype)


def token_gradients(z, idx, off, count, weight, pulled, maps, cots, n, rows, per):
    segs = idx.shape[0]
    width, keys = weight.shape
    sizes = [got[0].shape[0] for got in cots]
    ranks = maps[0].shape[1]
    total = sum(m.shape[0] for m in maps)
    return pl.pallas_call(
        functools.partial(token_kernel, n, per, rows, sizes, len(maps)),
        grid=(segs // per,),
        out_shape=jax.ShapeDtypeStruct((segs * rows, width), jnp.bfloat16),
        in_specs=[SMEM] * 4
        + [pl.BlockSpec(weight.shape, lambda i: (0, 0), pipeline_mode=pl.Buffered(1))]
        + [pl.BlockSpec((per * rows, ranks), lambda i: (i, 0))]
        + [ANY] * (len(maps) + n * len(sizes)),
        out_specs=pl.BlockSpec((per * rows, width), lambda i: (i, 0)),
        scratch_shapes=[
            pltpu.VMEM((total, ranks, width), jnp.bfloat16),
            pltpu.VMEM((sum(sizes) + rows, keys), jnp.bfloat16),
            pltpu.SemaphoreType.DMA((len(maps),)),
            pltpu.SemaphoreType.DMA((n * len(sizes),)),
        ],
        compiler_params=params(60),
        cost_estimate=cost(16),
        name="token_gradient",
    )(z, idx, off, count, weight, pulled, *maps, *[a for got in cots for a in got])


def gate_kernel(*refs):
    del refs


def gate(*arrays):
    return pl.pallas_call(
        gate_kernel,
        out_shape=[jax.ShapeDtypeStruct(a.shape, a.dtype) for a in arrays],
        in_specs=[ANY] * len(arrays),
        out_specs=[ANY] * len(arrays),
        input_output_aliases={i: i for i in range(len(arrays))},
        compiler_params=params(1),
        cost_estimate=cost(0),
        name="gate",
    )(*arrays)


def ring(x, n):
    return lax.ppermute(x, "tsp", [(i, (i + 1) % n) for i in range(n)])


def flip(x, n, by):
    return lax.ppermute(x, "dp", [(i, i ^ by) for i in range(n)])


def on_device(
    tokens,
    cotangent,
    frozen_key_weight,
    adapter_down_weight,
    adapter_up_weight,
    adapter_place_table,
    segment_adapter,
    segment_live_count,
):
    n_dp = lax.axis_size("dp")
    n = lax.axis_size("tsp")
    me = lax.axis_index("dp").astype(jnp.int32)
    z = lax.axis_index("tsp").astype(jnp.int32)[None]
    held = adapter_down_weight.shape[0]
    segs = segment_adapter.shape[0]
    rows = tokens.shape[0] // segs
    full = segs * rows
    cube = n_dp == 8 and held == 2

    places = lookup(segment_adapter, adapter_place_table)
    owner, entry = places // held, places % held
    peers = jnp.arange(n_dp, dtype=jnp.int32)
    wanted = jnp.max(jnp.where(owner[:, None] == peers[None, :], entry[:, None], -1), axis=0)
    count = segment_live_count
    padded = (count + 15) // 16 * 16
    off = jnp.cumsum(padded) - padded

    up_line = [
        lax.ppermute(adapter_up_weight, "tsp", [(i, (i + s) % n) for i in range(n)]) for s in range(1, n)
    ]
    whole = pack(cotangent, off, segs, [full], after=up_line)[0]
    up_line = jnp.stack([adapter_up_weight, *up_line])
    first = ring(whole, n)
    if cube:
        idx = (owner ^ me) * held + entry
        over_x, over_y = flip(adapter_down_weight, n_dp, 2), flip(adapter_down_weight, n_dp, 4)
        first, over_x, over_y = gate(first, over_x, over_y)
    else:
        idx = places

    def main(packed):
        cots = [whole, first]
        cots.append(ring(cots[-1], n))
        if cube:
            corner = [flip(over_x[:1], n_dp, 4), flip(over_y[1:], n_dp, 2)]
            same = [adapter_down_weight, over_x, over_y]
            other = [flip(m, n_dp, 1) for m in same]
            up_same = [flip(up_line, n_dp, k) for k in (2, 4, 6)]
            told = wanted[None]
            told = jnp.concatenate([told, flip(told, n_dp, 1)])
            *corner, ux, uy, ud, told = gate(*corner, *up_same, told)
            up_same = [up_line, ux, uy, ud]
            ups = [m for u in up_same for m in (u, flip(u, n_dp, 1))]
            far = [flip(m, n_dp, 1) for m in corner]
            downs = [m for pair in zip(same, other) for m in pair]
            downs += [jnp.concatenate(corner), jnp.concatenate(far)]
            told = jnp.concatenate([told] + [flip(told, n_dp, k) for k in (2, 4, 6)])
            asked = jnp.sum(jnp.where(peers[None, :] == me, told, 0), axis=1)[peers ^ me]
        else:
            ups = [lax.all_gather(up_line, "dp", axis=1, tiled=True)]
            downs = [lax.all_gather(adapter_down_weight, "dp", axis=0, tiled=True)]
            asked = lax.all_gather(wanted, "dp", axis=0, tiled=False)[:, me]
        lowered = project(idx, off, count, tokens, downs, n, packed, 4, 4)
        cots[2], lowered, asked = gate(cots[2], lowered, asked)
        parts = lax.all_to_all(lowered, "tsp", 0, 0, tiled=True)
        while len(cots) < n:
            cots.append(ring(cots[-1], n))
        cots[-1], parts = gate(cots[-1], parts)
        lowered = jnp.sum(parts, axis=0).astype(jnp.bfloat16)
        lowered = lax.all_to_all(jnp.broadcast_to(lowered, parts.shape), "tsp", 0, 0, tiled=True)

        sent, pulled = down_sums(
            z, idx, owner, off, count, tokens, ups, [cots], n_dp, n, 4, 7, cotangent.shape[1]
        )
        sent = up_sums(owner, off, count, cotangent, lowered, sent, 2)
        got = lax.all_to_all(sent, "dp", 0, 0, tiled=True)
        token_gradient = token_gradients(
            z, idx, off, count, frozen_key_weight, pulled, downs, [cots], n, rows, 2
        )
        hits = asked[None, :] == jnp.arange(held, dtype=jnp.int32)[:, None]
        grads = jnp.sum(jnp.where(hits[:, :, None, None], got.astype(jnp.float32)[None], 0.0), axis=1)
        width = tokens.shape[1]
        return token_gradient, grads[:, :, :width], grads[:, :, width:]

    return main(full)


def solution(mesh):
    placed = (
        P("dp", "tsp"),
        P("dp", "tsp"),
        P("tsp", None),
        P("dp", None, "tsp"),
        P("dp", None, "tsp"),
        P(),
        P("dp"),
        P("dp"),
    )
    return jax.shard_map(
        on_device,
        mesh=mesh,
        in_specs=placed,
        out_specs=(P("dp", "tsp"), P("dp", None, "tsp"), P("dp", None, "tsp")),
        check_vma=False,
    )
```

```python
import functools

import jax
import jax.numpy as jnp
from jax import lax
from jax.experimental import pallas as pl
from jax.experimental.pallas import tpu as pltpu
from jax.sharding import PartitionSpec as P

ADAPTER_SCALE = 2.0
HBM = pl.BlockSpec(memory_space=pltpu.HBM)
SMEM = pl.BlockSpec(memory_space=pltpu.SMEM)
VMEM = pl.BlockSpec(memory_space=pltpu.VMEM)
NT = (((1,), (1,)), ((), ()))
TN = (((0,), (0,)), ((), ()))
NN = (((1,), (0,)), ((), ()))
MIB = 1024 * 1024


def params(mib=60):
    return pltpu.CompilerParams(vmem_limit_bytes=mib * MIB)


def cost(us):
    return pl.CostEstimate(flops=0, bytes_accessed=int(us * 3e5), transcendentals=0)


def map_copies(maps, table, sem):
    copies, first = [], 0
    for i, m in enumerate(maps):
        copies.append(pltpu.make_async_copy(m, table.at[pl.ds(first, m.shape[0])], sem.at[i]))
        first += m.shape[0]
    return copies


def load_all(copies):
    for copy in copies:
        copy.start()
    for copy in copies:
        copy.wait()


def live_mask(count, rows, width):
    return lax.broadcasted_iota(jnp.int32, (rows, width), 0) < count


def plan_kernel(held, cube, me, table, adapter, owner, idx, wanted):
    for k in range(wanted.shape[0]):
        wanted[k] = -1
    for g in range(owner.shape[0]):
        place = table[adapter[g]]
        who = lax.div(place, held)
        owner[g] = who
        wanted[who] = lax.rem(place, held)
        idx[g] = lax.bitwise_xor(who, me[0]) * held + lax.rem(place, held) if cube else place


def plan(me, table, adapter, held, owners, cube):
    whole = lambda length: jax.ShapeDtypeStruct((length,), jnp.int32)
    segs = adapter.shape[0]
    return pl.pallas_call(
        functools.partial(plan_kernel, held, cube),
        out_shape=[whole(segs), whole(segs), whole(owners)],
        in_specs=[SMEM] * 3,
        out_specs=[SMEM] * 3,
        compiler_params=params(),
        cost_estimate=cost(1),
        name="plan",
    )(me, table, adapter)


def project_kernel(n, per, rows, n_maps, idx, count, x, *refs):
    maps, (out, table, buf, sem) = refs[:n_maps], refs[-4:]
    step = pl.program_id(0)

    @pl.when(step == 0)
    def _():
        load_all(map_copies(maps, table, sem))

    for i in range(per):
        g = step * per + i
        term = lax.dot_general(
            table[idx[g]], x[i * rows : (i + 1) * rows, :], NT, preferred_element_type=jnp.float32
        ).T
        term = jnp.where(live_mask(count[g], *term.shape), term, 0.0)
        buf[pl.ds(pl.multiple_of(g * rows, rows), rows), :] = term

    @pl.when(step == pl.num_programs(0) - 1)
    def _():
        half = out.shape[1]
        for j in range(n):
            start = 2 * j * half
            out[j] = jnp.concatenate(
                [buf[start : start + half, :], buf[start + half : start + 2 * half, :]], axis=1
            )


def project(idx, count, x, maps, n, per, us):
    segs = idx.shape[0]
    rows, width = x.shape[0] // segs, x.shape[1]
    ranks = maps[0].shape[1]
    total = sum(m.shape[0] for m in maps)
    shape = (n, x.shape[0] // n // 2, 2 * ranks)
    return pl.pallas_call(
        functools.partial(project_kernel, n, per, rows, len(maps)),
        grid=(segs // per,),
        out_shape=jax.ShapeDtypeStruct(shape, jnp.float32),
        in_specs=[SMEM] * 2 + [pl.BlockSpec((per * rows, width), lambda i: (i, 0))] + [HBM] * len(maps),
        out_specs=pl.BlockSpec(shape, lambda i: (0, 0, 0)),
        scratch_shapes=[
            pltpu.VMEM((total, ranks, width), x.dtype),
            pltpu.VMEM((x.shape[0], ranks), jnp.float32),
            pltpu.SemaphoreType.DMA((len(maps),)),
        ],
        compiler_params=params(),
        cost_estimate=cost(us),
        name="project",
    )(idx, count, x, *maps)


def cot_copies(n, z, cots, cot, sem):
    key = cots[0].shape[1]
    copies = []
    for s in range(n):
        column = pl.multiple_of(lax.rem(z - s + n, n) * key, key)
        copies.append(pltpu.make_async_copy(cots[s], cot.at[:, pl.ds(column, key)], sem.at[s]))
    return copies


def add_terms(total, owner, terms, x):
    total[owner] += lax.dot_general(terms, x, TN, preferred_element_type=jnp.float32)


def up_sums_kernel(n, rows, scale, z, owner, x_hbm, *refs):
    blocks, (out, x, raw, buf, total, sem) = refs[:n], refs[-6:]
    half, ranks = raw.shape[1], raw.shape[2] // 2
    copies = [pltpu.make_async_copy(x_hbm, x, sem.at[n])]
    for s in range(n):
        copies.append(pltpu.make_async_copy(blocks[s], raw.at[lax.rem(z[0] - s + n, n)], sem.at[s]))
    for copy in copies:
        copy.start()
    total[...] = jnp.zeros_like(total)
    for copy in copies:
        copy.wait()
    for j in range(n):
        start = 2 * j * half
        buf[start : start + half, :] = raw[j][:, :ranks]
        buf[start + half : start + 2 * half, :] = raw[j][:, ranks:]
    for g in range(x.shape[0] // rows):
        add_terms(total, owner[g], buf[g * rows : (g + 1) * rows, :], x[g * rows : (g + 1) * rows, :])
    out[...] = (total[...] * scale).astype(out.dtype)


def up_sums(z, owner, x, blocks, owners, us, after=()):
    segs, n = owner.shape[0], len(blocks)
    rows, width = x.shape[0] // segs, x.shape[1]
    ranks = blocks[0].shape[1] // 2
    shape = (owners, ranks, width)
    return pl.pallas_call(
        functools.partial(up_sums_kernel, n, rows, ADAPTER_SCALE / rows),
        out_shape=jax.ShapeDtypeStruct(shape, jnp.bfloat16),
        in_specs=[SMEM] * 2 + [HBM] * (1 + n + len(after)),
        out_specs=VMEM,
        scratch_shapes=[
            pltpu.VMEM(x.shape, x.dtype),
            pltpu.VMEM((n, *blocks[0].shape), jnp.bfloat16),
            pltpu.VMEM((x.shape[0], ranks), jnp.bfloat16),
            pltpu.VMEM(shape, jnp.float32),
            pltpu.SemaphoreType.DMA((n + 1,)),
        ],
        compiler_params=params(),
        cost_estimate=cost(us),
        name="up_sums",
    )(z, owner, x, *blocks, *after)


def down_sums_kernel(n, per, rows, n_maps, scale, z, idx, owner, count, x, *refs):
    maps, refs = refs[:n_maps], refs[n_maps:]
    cots, (out, pulled, table, cot, total, map_sem, cot_sem) = refs[:n], refs[-7:]
    step = pl.program_id(0)

    @pl.when(step == 0)
    def _():
        copies = cot_copies(n, z[0], cots, cot, cot_sem)
        parts, held, _, key = maps[0].shape
        for i, m in enumerate(maps):
            for j in range(parts):
                column = pl.multiple_of(lax.rem(z[0] - j + n, n) * key, key)
                dst = table.at[pl.ds(i * held, held), :, pl.ds(column, key)]
                copies.append(pltpu.make_async_copy(m.at[j], dst, map_sem.at[i * parts + j]))
        for copy in copies:
            copy.start()
        total[...] = jnp.zeros_like(total)
        for copy in copies:
            copy.wait()

    for i in range(per):
        g = step * per + i
        terms = lax.dot_general(
            cot[pl.ds(pl.multiple_of(g * rows, rows), rows), :],
            table[idx[g]],
            NT,
            preferred_element_type=jnp.float32,
        )
        terms = jnp.where(live_mask(count[g], *terms.shape), terms, 0.0).astype(pulled.dtype)
        pulled[i * rows : (i + 1) * rows, :] = terms
        add_terms(total, owner[g], terms, x[i * rows : (i + 1) * rows, :])

    @pl.when(step == pl.num_programs(0) - 1)
    def _():
        out[...] = (total[...] * scale).astype(out.dtype)


def down_sums(z, idx, owner, count, x, maps, cots, owners, n, per, us):
    segs = owner.shape[0]
    rows, width = x.shape[0] // segs, x.shape[1]
    parts, held, ranks, key = maps[0].shape
    shape = (owners, ranks, width)
    return pl.pallas_call(
        functools.partial(down_sums_kernel, n, per, rows, len(maps), ADAPTER_SCALE / rows),
        grid=(segs // per,),
        out_shape=[
            jax.ShapeDtypeStruct(shape, jnp.bfloat16),
            jax.ShapeDtypeStruct((x.shape[0], ranks), jnp.bfloat16),
        ],
        in_specs=[SMEM] * 4
        + [pl.BlockSpec((per * rows, width), lambda i: (i, 0))]
        + [HBM] * (len(maps) + n),
        out_specs=[
            pl.BlockSpec(shape, lambda i: (0, 0, 0)),
            pl.BlockSpec((per * rows, ranks), lambda i: (i, 0)),
        ],
        scratch_shapes=[
            pltpu.VMEM((held * len(maps), ranks, parts * key), jnp.bfloat16),
            pltpu.VMEM((x.shape[0], n * key), jnp.bfloat16),
            pltpu.VMEM(shape, jnp.float32),
            pltpu.SemaphoreType.DMA((parts * len(maps),)),
            pltpu.SemaphoreType.DMA((n,)),
        ],
        compiler_params=params(),
        cost_estimate=cost(us),
        name="down_sums",
    )(z, idx, owner, count, x, *maps, *cots)


def token_kernel(n, per, rows, n_maps, z, idx, count, weight, pulled, *refs):
    maps, refs = refs[:n_maps], refs[n_maps:]
    cots, (out, table, cot, map_sem, cot_sem) = refs[:n], refs[-5:]
    step = pl.program_id(0)

    @pl.when(step == 0)
    def _():
        load_all(cot_copies(n, z[0], cots, cot, cot_sem) + map_copies(maps, table, map_sem))

    width = weight.shape[1]
    tile = min(512, width)
    counts = [count[step * per + i] for i in range(per)]
    x = cot[pl.ds(pl.multiple_of(step * per * rows, per * rows), per * rows), :]
    for d in range(0, width, tile):
        total = lax.dot_general(x, weight[:, d : d + tile], NN, preferred_element_type=jnp.float32)
        for i in range(per):
            adapter = lax.dot_general(
                pulled[i * rows : (i + 1) * rows, :],
                table[idx[step * per + i], :, d : d + tile],
                NN,
                preferred_element_type=jnp.float32,
            )
            both = total[i * rows : (i + 1) * rows, :] + ADAPTER_SCALE * adapter
            both = jnp.where(live_mask(counts[i], rows, tile), both, 0.0)
            out[i * rows : (i + 1) * rows, d : d + tile] = both.astype(out.dtype)


def token_gradients(z, idx, count, weight, pulled, maps, cots, n, rows, per, after=()):
    segs = idx.shape[0]
    keys, width = weight.shape
    ranks = maps[0].shape[1]
    total = sum(m.shape[0] for m in maps)
    return pl.pallas_call(
        functools.partial(token_kernel, n, per, rows, len(maps)),
        grid=(segs // per,),
        out_shape=jax.ShapeDtypeStruct((segs * rows, width), jnp.bfloat16),
        in_specs=[SMEM] * 3
        + [pl.BlockSpec(weight.shape, lambda i: (0, 0), pipeline_mode=pl.Buffered(1))]
        + [pl.BlockSpec((per * rows, ranks), lambda i: (i, 0))]
        + [HBM] * (len(maps) + n + len(after)),
        out_specs=pl.BlockSpec((per * rows, width), lambda i: (i, 0)),
        scratch_shapes=[
            pltpu.VMEM((total, ranks, width), jnp.bfloat16),
            pltpu.VMEM((segs * rows, keys), jnp.bfloat16),
            pltpu.SemaphoreType.DMA((len(maps),)),
            pltpu.SemaphoreType.DMA((n,)),
        ],
        compiler_params=params(),
        cost_estimate=cost(16),
        name="token_gradient",
    )(z, idx, count, weight, pulled, *maps, *cots, *after)


def owned_kernel(asked, got, out):
    for e in range(out.shape[0]):
        total = jnp.zeros(got.shape[1:], jnp.float32)
        for k in range(got.shape[0]):
            total += jnp.where(asked[k] == e, got[k].astype(jnp.float32), 0.0)
        out[e] = total


def owned(asked, got, held, mib):
    peers, ranks, width = got.shape
    per = min(16, ranks)
    return pl.pallas_call(
        owned_kernel,
        grid=(ranks // per,),
        out_shape=jax.ShapeDtypeStruct((held, ranks, width), jnp.float32),
        in_specs=[SMEM, pl.BlockSpec((peers, per, width), lambda i: (0, i, 0))],
        out_specs=pl.BlockSpec((held, per, width), lambda i: (0, i, 0)),
        compiler_params=params(mib),
        cost_estimate=cost(2),
        name="owned",
    )(asked, got)


def gate_kernel(*refs):
    del refs


def gate(*arrays, after=()):
    return pl.pallas_call(
        gate_kernel,
        out_shape=[jax.ShapeDtypeStruct(a.shape, a.dtype) for a in arrays],
        in_specs=[HBM] * (len(arrays) + len(after)),
        out_specs=[HBM] * len(arrays),
        input_output_aliases={i: i for i in range(len(arrays))},
        compiler_params=params(),
        cost_estimate=cost(0),
        name="gate",
    )(*arrays, *after)


def ring(x, n):
    return lax.ppermute(x, "tsp", [(i, (i + 1) % n) for i in range(n)])


def flip(x, n, by):
    return lax.ppermute(x, "dp", [(i, i ^ by) for i in range(n)])


def on_device(
    tokens,
    cotangent,
    frozen_key_weight,
    adapter_down_weight,
    adapter_up_weight,
    adapter_place_table,
    segment_adapter,
    segment_live_count,
):
    n_dp = lax.axis_size("dp")
    n = lax.axis_size("tsp")
    me = lax.axis_index("dp").astype(jnp.int32)
    z = lax.axis_index("tsp").astype(jnp.int32)[None]
    held = adapter_down_weight.shape[0]
    segs = segment_adapter.shape[0]
    rows = tokens.shape[0] // segs
    full = segs * rows
    cube = n_dp == 8 and held == 2

    peers = jnp.arange(n_dp, dtype=jnp.int32)
    count = segment_live_count
    ups, downs = adapter_up_weight, adapter_down_weight

    cots = [cotangent, ring(cotangent, n)]
    owner, idx, wanted = plan(me[None], adapter_place_table, segment_adapter, held, n_dp, cube)
    if cube:
        over_x, over_y = gate(flip(downs, n_dp, 2), flip(downs, n_dp, 4))
        ups = gate(ups, after=[over_x, over_y])[0]
    line = [lax.ppermute(ups, "tsp", [(i, (i + s) % n) for i in range(n)]) for s in range(1, n)]
    weight = frozen_key_weight.T
    if cube:
        cots[1], ups, weight, over_x, over_y, *line = gate(cots[1], ups, weight, over_x, over_y, *line)
        corner = [flip(over_x[:1], n_dp, 4), flip(over_y[1:], n_dp, 2)]
    else:
        cots[1], ups, weight, *line = gate(cots[1], ups, weight, *line)

    while len(cots) < n - 1:
        cots.append(ring(cots[-1], n))
    up_line = jnp.stack([ups, *line])
    if cube:
        same = [downs, over_x, over_y]
        downs_here = [m for d in same for m in (d, flip(d, n_dp, 1))]
        downs_here += corner + [flip(m, n_dp, 1) for m in corner]
    else:
        downs_here = [lax.all_gather(downs, "dp", axis=0, tiled=True)]
    lowered = project(idx, count, tokens, downs_here, n, 4, 4)
    cots[-1], up_line = gate(cots[-1], up_line, after=[lowered])

    cots.append(ring(cots[-1], n))
    if cube:
        same = [up_line] + [flip(up_line, n_dp, k) for k in (2, 4, 6)]
        all_ups = [m for u in same for m in (u, flip(u, n_dp, 1))]
        word = jnp.stack([wanted, flip(wanted, n_dp, 1)])
        words = jnp.concatenate([word] + [flip(word, n_dp, k) for k in (2, 4, 6)])
        asked = jnp.sum(jnp.where(peers[None, :] == me, words, 0), axis=1)[peers ^ me]
    else:
        all_ups = [lax.all_gather(up_line, "dp", axis=1, tiled=True)]
        asked = lax.all_gather(wanted, "dp", axis=0, tiled=False)[:, me]
    cots[-1], lowered = gate(cots[-1], lowered, after=[*all_ups, asked])

    parts = lax.all_to_all(lowered, "tsp", 0, 0, tiled=True)
    sent, pulled = down_sums(z, idx, owner, count, tokens, all_ups, cots, n_dp, n, 4, 7)
    down_got = lax.all_to_all(sent, "dp", 0, 0, tiled=True)
    token_gradient = token_gradients(
        z, idx, count, weight, pulled, downs_here, cots, n, rows, 4, after=[parts]
    )
    parts = gate(parts, after=[token_gradient])[0]
    lowered = jnp.sum(parts, axis=0).astype(jnp.bfloat16)
    lowered = [lowered] + [
        lax.ppermute(lowered, "tsp", [(i, (i + s) % n) for i in range(n)]) for s in range(1, n)
    ]
    sent = up_sums(z, owner, cotangent, lowered, n_dp, 2)
    sent = gate(sent, after=[down_got])[0]
    up_got = lax.all_to_all(sent, "dp", 0, 0, tiled=True)
    return token_gradient, owned(asked, down_got, held, 60), owned(asked, up_got, held, 16)


def solution(mesh):
    placed = (
        P("dp", "tsp"),
        P("dp", "tsp"),
        P("tsp", None),
        P("dp", None, "tsp"),
        P("dp", None, "tsp"),
        P(),
        P("dp"),
        P("dp"),
    )
    return jax.shard_map(
        on_device,
        mesh=mesh,
        in_specs=placed,
        out_specs=(P("dp", "tsp"), P("dp", None, "tsp"), P("dp", None, "tsp")),
        check_vma=False,
    )
```

```python
import functools

import jax
import jax.numpy as jnp
from jax import lax
from jax.experimental import pallas as pl
from jax.experimental.pallas import tpu as pltpu
from jax.sharding import PartitionSpec as P

ADAPTER_SCALE = 2.0
HBM = pl.BlockSpec(memory_space=pltpu.HBM)
SMEM = pl.BlockSpec(memory_space=pltpu.SMEM)
VMEM = pl.BlockSpec(memory_space=pltpu.VMEM)
NT = (((1,), (1,)), ((), ()))
TN = (((0,), (0,)), ((), ()))
NN = (((1,), (0,)), ((), ()))
MIB = 1024 * 1024


def params(mib=60):
    return pltpu.CompilerParams(vmem_limit_bytes=mib * MIB)


def cost(us):
    return pl.CostEstimate(flops=0, bytes_accessed=int(us * 3e5), transcendentals=0)


def map_copies(maps, table, sem):
    copies, first = [], 0
    for i, m in enumerate(maps):
        copies.append(pltpu.make_async_copy(m, table.at[pl.ds(first, m.shape[0])], sem.at[i]))
        first += m.shape[0]
    return copies


def load_all(copies):
    for copy in copies:
        copy.start()
    for copy in copies:
        copy.wait()


def live_mask(count, rows, width):
    return lax.broadcasted_iota(jnp.int32, (rows, width), 0) < count


def plan_kernel(held, cube, me, table, adapter, owner, idx, wanted):
    for k in range(wanted.shape[0]):
        wanted[k] = -1
    for g in range(owner.shape[0]):
        place = table[adapter[g]]
        who = lax.div(place, held)
        owner[g] = who
        wanted[who] = lax.rem(place, held)
        idx[g] = lax.bitwise_xor(who, me[0]) * held + lax.rem(place, held) if cube else place


def plan(me, table, adapter, held, owners, cube):
    whole = lambda length: jax.ShapeDtypeStruct((length,), jnp.int32)
    segs = adapter.shape[0]
    return pl.pallas_call(
        functools.partial(plan_kernel, held, cube),
        out_shape=[whole(segs), whole(segs), whole(owners)],
        in_specs=[SMEM] * 3,
        out_specs=[SMEM] * 3,
        compiler_params=params(),
        cost_estimate=cost(1),
        name="plan",
    )(me, table, adapter)


def project_kernel(n, per, rows, n_maps, z, idx, count, x, *refs):
    maps, outs, (table, buf, sem) = refs[:n_maps], refs[n_maps : n_maps + n], refs[-3:]
    step = pl.program_id(0)

    @pl.when(step == 0)
    def _():
        load_all(map_copies(maps, table, sem))

    for i in range(per):
        g = step * per + i
        term = lax.dot_general(
            table[idx[g]], x[i * rows : (i + 1) * rows, :], NT, preferred_element_type=jnp.float32
        ).T
        term = jnp.where(live_mask(count[g], *term.shape), term, 0.0)
        buf[pl.ds(pl.multiple_of(g * rows, rows), rows), :] = term

    @pl.when(step == pl.num_programs(0) - 1)
    def _():
        half = outs[0].shape[0]
        for s in range(n):
            start = pl.multiple_of(lax.rem(z[0] + s, n) * 2 * half, 2 * half)
            outs[s][...] = jnp.concatenate(
                [buf[pl.ds(start, half), :], buf[pl.ds(start + half, half), :]], axis=1
            )


def project(z, idx, count, x, maps, n, per, us):
    segs = idx.shape[0]
    rows, width = x.shape[0] // segs, x.shape[1]
    ranks = maps[0].shape[1]
    total = sum(m.shape[0] for m in maps)
    shape = (x.shape[0] // n // 2, 2 * ranks)
    return pl.pallas_call(
        functools.partial(project_kernel, n, per, rows, len(maps)),
        grid=(segs // per,),
        out_shape=[jax.ShapeDtypeStruct(shape, jnp.float32)] * n,
        in_specs=[SMEM] * 3 + [pl.BlockSpec((per * rows, width), lambda i: (i, 0))] + [HBM] * len(maps),
        out_specs=[pl.BlockSpec(shape, lambda i: (0, 0))] * n,
        scratch_shapes=[
            pltpu.VMEM((total, ranks, width), x.dtype),
            pltpu.VMEM((x.shape[0], ranks), jnp.float32),
            pltpu.SemaphoreType.DMA((len(maps),)),
        ],
        compiler_params=params(),
        cost_estimate=cost(us),
        name="project",
    )(z, idx, count, x, *maps)


def cot_copies(n, z, cots, cot, sem):
    key = cots[0].shape[1]
    copies = []
    for s in range(n):
        column = pl.multiple_of(lax.rem(z - s + n, n) * key, key)
        copies.append(pltpu.make_async_copy(cots[s], cot.at[:, pl.ds(column, key)], sem.at[s]))
    return copies


def add_terms(total, owner, terms, x):
    total[owner] += lax.dot_general(terms, x, TN, preferred_element_type=jnp.float32)


def up_sums_kernel(n, rows, scale, z, owner, x_hbm, *refs):
    blocks, (out, x, raw, buf, total, sem) = refs[:n], refs[-6:]
    half, ranks = raw.shape[1], raw.shape[2] // 2
    copies = [pltpu.make_async_copy(x_hbm, x, sem.at[n])]
    for s in range(n):
        copies.append(pltpu.make_async_copy(blocks[s], raw.at[lax.rem(z[0] - s + n, n)], sem.at[s]))
    for copy in copies:
        copy.start()
    total[...] = jnp.zeros_like(total)
    for copy in copies:
        copy.wait()
    for j in range(n):
        start = 2 * j * half
        buf[start : start + half, :] = raw[j][:, :ranks]
        buf[start + half : start + 2 * half, :] = raw[j][:, ranks:]
    for g in range(x.shape[0] // rows):
        add_terms(total, owner[g], buf[g * rows : (g + 1) * rows, :], x[g * rows : (g + 1) * rows, :])
    out[...] = (total[...] * scale).astype(out.dtype)


def up_sums(z, owner, x, blocks, owners, us, after=()):
    segs, n = owner.shape[0], len(blocks)
    rows, width = x.shape[0] // segs, x.shape[1]
    ranks = blocks[0].shape[1] // 2
    shape = (owners, ranks, width)
    return pl.pallas_call(
        functools.partial(up_sums_kernel, n, rows, ADAPTER_SCALE / rows),
        out_shape=jax.ShapeDtypeStruct(shape, jnp.bfloat16),
        in_specs=[SMEM] * 2 + [HBM] * (1 + n + len(after)),
        out_specs=VMEM,
        scratch_shapes=[
            pltpu.VMEM(x.shape, x.dtype),
            pltpu.VMEM((n, *blocks[0].shape), jnp.bfloat16),
            pltpu.VMEM((x.shape[0], ranks), jnp.bfloat16),
            pltpu.VMEM(shape, jnp.float32),
            pltpu.SemaphoreType.DMA((n + 1,)),
        ],
        compiler_params=params(),
        cost_estimate=cost(us),
        name="up_sums",
    )(z, owner, x, *blocks, *after)


def up_copies(maps, size, distances, table, sem):
    key = maps[0].shape[1]
    copies = []
    for i, m in enumerate(maps):
        for k, j in enumerate(distances):
            dst = table.at[pl.ds(i * size, size), pl.ds(k * key, key)]
            copies.append(pltpu.make_async_copy(m.at[pl.ds(j * size, size)], dst, sem.at[i * len(distances) + k]))
    return copies


def pick(place, ranks):
    return pl.ds(pl.multiple_of(place * ranks, ranks), ranks)


def pulled_part_kernel(n, per, rows, ranks, size, n_maps, idx, *refs):
    cots, maps, (out, table, sem) = refs[: n - 1], refs[n - 1 : n - 1 + n_maps], refs[-3:]
    step = pl.program_id(0)

    @pl.when(step == 0)
    def _():
        load_all(up_copies(maps, size, range(n - 1), table, sem))

    for i in range(per):
        x = jnp.concatenate([cot[i * rows : (i + 1) * rows, :] for cot in cots], axis=1)
        out[i * rows : (i + 1) * rows, :] = lax.dot_general(
            x, table[pick(idx[step * per + i], ranks), :], NT, preferred_element_type=jnp.float32
        )


def pulled_part(idx, maps, cots, ranks, size, per, us):
    segs, n = idx.shape[0], len(cots) + 1
    rows, key = cots[0].shape[0] // segs, cots[0].shape[1]
    return pl.pallas_call(
        functools.partial(pulled_part_kernel, n, per, rows, ranks, size, len(maps)),
        grid=(segs // per,),
        out_shape=jax.ShapeDtypeStruct((segs * rows, ranks), jnp.float32),
        in_specs=[SMEM]
        + [pl.BlockSpec((per * rows, key), lambda i: (i, 0))] * (n - 1)
        + [HBM] * len(maps),
        out_specs=pl.BlockSpec((per * rows, ranks), lambda i: (i, 0)),
        scratch_shapes=[
            pltpu.VMEM((size * len(maps), (n - 1) * key), jnp.bfloat16),
            pltpu.SemaphoreType.DMA(((n - 1) * len(maps),)),
        ],
        compiler_params=params(),
        cost_estimate=cost(us),
        name="pulled_part",
    )(idx, *cots, *maps)


def down_sums_kernel(n, per, rows, ranks, size, n_maps, scale, idx, owner, count, x, part, cot, *refs):
    maps, (out, pulled, table, total, sem) = refs[:n_maps], refs[-5:]
    step = pl.program_id(0)

    @pl.when(step == 0)
    def _():
        copies = up_copies(maps, size, [n - 1], table, sem)
        for copy in copies:
            copy.start()
        total[...] = jnp.zeros_like(total)
        for copy in copies:
            copy.wait()

    for i in range(per):
        g = step * per + i
        terms = part[i * rows : (i + 1) * rows, :] + lax.dot_general(
            cot[i * rows : (i + 1) * rows, :], table[pick(idx[g], ranks), :], NT, preferred_element_type=jnp.float32
        )
        terms = jnp.where(live_mask(count[g], *terms.shape), terms, 0.0).astype(pulled.dtype)
        pulled[i * rows : (i + 1) * rows, :] = terms
        add_terms(total, owner[g], terms, x[i * rows : (i + 1) * rows, :])

    @pl.when(step == pl.num_programs(0) - 1)
    def _():
        out[...] = (total[...] * scale).astype(out.dtype)


def down_sums(idx, owner, count, x, part, cot, maps, size, owners, n, per, us):
    segs = owner.shape[0]
    rows, width = x.shape[0] // segs, x.shape[1]
    ranks, key = part.shape[1], cot.shape[1]
    shape = (owners, ranks, width)
    by_rows = lambda columns: pl.BlockSpec((per * rows, columns), lambda i: (i, 0))
    return pl.pallas_call(
        functools.partial(down_sums_kernel, n, per, rows, ranks, size, len(maps), ADAPTER_SCALE / rows),
        grid=(segs // per,),
        out_shape=[
            jax.ShapeDtypeStruct(shape, jnp.bfloat16),
            jax.ShapeDtypeStruct((x.shape[0], ranks), jnp.bfloat16),
        ],
        in_specs=[SMEM] * 3 + [by_rows(width), by_rows(ranks), by_rows(key)] + [HBM] * len(maps),
        out_specs=[pl.BlockSpec(shape, lambda i: (0, 0, 0)), by_rows(ranks)],
        scratch_shapes=[
            pltpu.VMEM((size * len(maps), key), jnp.bfloat16),
            pltpu.VMEM(shape, jnp.float32),
            pltpu.SemaphoreType.DMA((len(maps),)),
        ],
        compiler_params=params(),
        cost_estimate=cost(us),
        name="down_sums",
    )(idx, owner, count, x, part, cot, *maps)


def token_kernel(n, per, rows, n_maps, z, idx, count, weight, pulled, *refs):
    maps, refs = refs[:n_maps], refs[n_maps:]
    cots, (out, table, cot, map_sem, cot_sem) = refs[:n], refs[-5:]
    step = pl.program_id(0)

    @pl.when(step == 0)
    def _():
        load_all(cot_copies(n, z[0], cots, cot, cot_sem) + map_copies(maps, table, map_sem))

    width = weight.shape[1]
    tile = min(512, width)
    counts = [count[step * per + i] for i in range(per)]
    x = cot[pl.ds(pl.multiple_of(step * per * rows, per * rows), per * rows), :]
    for d in range(0, width, tile):
        total = lax.dot_general(x, weight[:, d : d + tile], NN, preferred_element_type=jnp.float32)
        for i in range(per):
            adapter = lax.dot_general(
                pulled[i * rows : (i + 1) * rows, :],
                table[idx[step * per + i], :, d : d + tile],
                NN,
                preferred_element_type=jnp.float32,
            )
            both = total[i * rows : (i + 1) * rows, :] + ADAPTER_SCALE * adapter
            both = jnp.where(live_mask(counts[i], rows, tile), both, 0.0)
            out[i * rows : (i + 1) * rows, d : d + tile] = both.astype(out.dtype)


def token_gradients(z, idx, count, weight, pulled, maps, cots, n, rows, per, after=()):
    segs = idx.shape[0]
    keys, width = weight.shape
    ranks = maps[0].shape[1]
    total = sum(m.shape[0] for m in maps)
    return pl.pallas_call(
        functools.partial(token_kernel, n, per, rows, len(maps)),
        grid=(segs // per,),
        out_shape=jax.ShapeDtypeStruct((segs * rows, width), jnp.bfloat16),
        in_specs=[SMEM] * 3
        + [pl.BlockSpec(weight.shape, lambda i: (0, 0), pipeline_mode=pl.Buffered(1))]
        + [pl.BlockSpec((per * rows, ranks), lambda i: (i, 0))]
        + [HBM] * (len(maps) + n + len(after)),
        out_specs=pl.BlockSpec((per * rows, width), lambda i: (i, 0)),
        scratch_shapes=[
            pltpu.VMEM((total, ranks, width), jnp.bfloat16),
            pltpu.VMEM((segs * rows, keys), jnp.bfloat16),
            pltpu.SemaphoreType.DMA((len(maps),)),
            pltpu.SemaphoreType.DMA((n,)),
        ],
        compiler_params=params(),
        cost_estimate=cost(16),
        name="token_gradient",
    )(z, idx, count, weight, pulled, *maps, *cots, *after)


def told_kernel(row, me, *refs):
    arrays, (out, raw, sem) = refs[:-3], refs[-3:]
    load_all([pltpu.make_async_copy(m.at[pl.ds(row, 16)], raw.at[i], sem.at[i]) for i, m in enumerate(arrays)])
    for i in range(len(arrays)):
        codes = raw[i][:8, :].astype(jnp.float32)
        mine = lax.broadcasted_iota(jnp.int32, codes.shape, 1) == me[0]
        code = jnp.sum(jnp.where(mine, codes, 0.0), axis=1, keepdims=True)
        out[i : i + 1, :] = jnp.broadcast_to(code, (codes.shape[0], out.shape[1]))[:1, :]


def told(me, arrays, row):
    return pl.pallas_call(
        functools.partial(told_kernel, row),
        out_shape=jax.ShapeDtypeStruct((len(arrays), 128), jnp.float32),
        in_specs=[SMEM] + [HBM] * len(arrays),
        out_specs=VMEM,
        scratch_shapes=[
            pltpu.VMEM((len(arrays), 16, arrays[0].shape[1]), arrays[0].dtype),
            pltpu.SemaphoreType.DMA((len(arrays),)),
        ],
        compiler_params=params(),
        cost_estimate=cost(1),
        name="told",
    )(me, *arrays)


def owned_kernel(first, asked, got, out):
    for e in range(out.shape[0]):
        total = jnp.zeros(got.shape[1:], jnp.float32)
        for k in range(got.shape[0]):
            code = asked[pl.ds(lax.bitwise_xor(first[0], k), 1), :1]
            total += jnp.where(code == jnp.float32(e), got[k].astype(jnp.float32), 0.0)
        out[e] = total


def owned(first, asked, got, held, mib):
    peers, ranks, width = got.shape
    per = min(16, ranks)
    return pl.pallas_call(
        owned_kernel,
        grid=(ranks // per,),
        out_shape=jax.ShapeDtypeStruct((held, ranks, width), jnp.float32),
        in_specs=[SMEM, VMEM, pl.BlockSpec((peers, per, width), lambda i: (0, i, 0))],
        out_specs=pl.BlockSpec((held, per, width), lambda i: (0, i, 0)),
        compiler_params=params(mib),
        cost_estimate=cost(2),
        name="owned",
    )(first, asked, got)


def gate_kernel(*refs):
    del refs


def gate(*arrays, after=()):
    return pl.pallas_call(
        gate_kernel,
        out_shape=[jax.ShapeDtypeStruct(a.shape, a.dtype) for a in arrays],
        in_specs=[HBM] * (len(arrays) + len(after)),
        out_specs=[HBM] * len(arrays),
        input_output_aliases={i: i for i in range(len(arrays))},
        compiler_params=params(),
        cost_estimate=cost(0),
        name="gate",
    )(*arrays, *after)


def late_kernel(x, *refs):
    out, sem = refs[-2:]
    load_all([pltpu.make_async_copy(x, out, sem)])


def late(x, after):
    return pl.pallas_call(
        late_kernel,
        out_shape=jax.ShapeDtypeStruct(x.shape, x.dtype),
        in_specs=[HBM] * (1 + len(after)),
        out_specs=HBM,
        scratch_shapes=[pltpu.SemaphoreType.DMA(())],
        compiler_params=params(),
        cost_estimate=cost(0),
        name="late",
    )(x, *after)


def ring(x, n):
    return lax.ppermute(x, "tsp", [(i, (i + 1) % n) for i in range(n)])


def flip(x, n, by):
    return lax.ppermute(x, "dp", [(i, i ^ by) for i in range(n)])


def on_device(
    tokens,
    cotangent,
    frozen_key_weight,
    adapter_down_weight,
    adapter_up_weight,
    adapter_place_table,
    segment_adapter,
    segment_live_count,
):
    n_dp = lax.axis_size("dp")
    n = lax.axis_size("tsp")
    me = lax.axis_index("dp").astype(jnp.int32)
    z = lax.axis_index("tsp").astype(jnp.int32)[None]
    held = adapter_down_weight.shape[0]
    segs = segment_adapter.shape[0]
    rows = tokens.shape[0] // segs
    full = segs * rows
    cube = n_dp == 8 and held == 2

    peers = jnp.arange(n_dp, dtype=jnp.int32)
    count = segment_live_count
    ups, downs = adapter_up_weight, adapter_down_weight

    cots = [cotangent, ring(cotangent, n)]
    owner, idx, wanted = plan(me[None], adapter_place_table, segment_adapter, held, n_dp, cube)
    if cube:
        over_x, over_y = gate(flip(downs, n_dp, 2), flip(downs, n_dp, 4))
        ups = late(ups, [over_x, over_y])
    line = [lax.ppermute(ups, "tsp", [(i, (i + s) % n) for i in range(n)]) for s in range(1, n)]
    weight = frozen_key_weight.T
    if cube:
        cots[1], ups, weight, over_x, over_y, *line = gate(cots[1], ups, weight, over_x, over_y, *line)
        corner = [flip(over_x[:1], n_dp, 4), flip(over_y[1:], n_dp, 2)]
    else:
        cots[1], ups, weight, *line = gate(cots[1], ups, weight, *line)

    while len(cots) < n - 1:
        cots.append(ring(cots[-1], n))
    ranks = ups.shape[1]
    size = held * ranks
    info = jnp.zeros((16, ups.shape[2]), ups.dtype).at[0, :n_dp].set(wanted.astype(ups.dtype))
    up_line = jnp.concatenate([u.reshape(size, -1) for u in [ups, *line]] + [info])
    if cube:
        same = [downs, over_x, over_y]
        downs_here = [m for d in same for m in (d, flip(d, n_dp, 1))]
        downs_here += corner + [flip(m, n_dp, 1) for m in corner]
    else:
        downs_here = [lax.all_gather(downs, "dp", axis=0, tiled=True)]
    lowered = project(z, idx, count, tokens, downs_here, n, 4, 4)
    cots[-1], up_line = gate(cots[-1], up_line, after=[lowered[0]])

    cots.append(ring(cots[-1], n))
    if cube:
        same = [up_line] + [flip(up_line, n_dp, k) for k in (2, 4, 6)]
        all_ups = [m for u in same for m in (u, flip(u, n_dp, 1))]
        origin = me[None]
    else:
        all_ups = [lax.all_gather(up_line, "dp", axis=0, tiled=False)[k] for k in range(n_dp)]
        origin = jnp.zeros((1,), jnp.int32)
    asked = told(me[None], all_ups, n * size)
    part = pulled_part(idx, all_ups, cots[:-1], ranks, size, 4, 5)
    cots[-1], *lowered = gate(cots[-1], *lowered, after=[part])

    shift = lambda x, s: lax.ppermute(x, "tsp", [(i, (i + s) % n) for i in range(n)]) if s else x
    parts = [shift(block, s) for s, block in enumerate(lowered)]
    sent, pulled = down_sums(idx, owner, count, tokens, part, cots[-1], all_ups, size, n_dp, n, 4, 7)
    sent = gate(sent, after=parts)[0]
    down_got = lax.all_to_all(sent, "dp", 0, 0, tiled=True)
    token_gradient = token_gradients(
        z, idx, count, weight, pulled, downs_here, cots, n, rows, 4
    )
    parts = gate(*parts, after=[token_gradient])
    lowered = functools.reduce(jnp.add, parts).astype(jnp.bfloat16)
    lowered = [shift(lowered, s) for s in range(n)]
    sent = up_sums(z, owner, cotangent, lowered, n_dp, 2)
    sent = gate(sent, after=[down_got])[0]
    up_got = lax.all_to_all(sent, "dp", 0, 0, tiled=True)
    return token_gradient, owned(origin, asked, down_got, held, 60), owned(origin, asked, up_got, held, 16)


def solution(mesh):
    placed = (
        P("dp", "tsp"),
        P("dp", "tsp"),
        P("tsp", None),
        P("dp", None, "tsp"),
        P("dp", None, "tsp"),
        P(),
        P("dp"),
        P("dp"),
    )
    return jax.shard_map(
        on_device,
        mesh=mesh,
        in_specs=placed,
        out_specs=(P("dp", "tsp"), P("dp", None, "tsp"), P("dp", None, "tsp")),
        check_vma=False,
    )
```

```python
import functools

import jax
import jax.numpy as jnp
from jax import lax
from jax.experimental import pallas as pl
from jax.experimental.pallas import tpu as pltpu
from jax.sharding import PartitionSpec as P

ADAPTER_SCALE = 2.0
HBM = pl.BlockSpec(memory_space=pltpu.HBM)
SMEM = pl.BlockSpec(memory_space=pltpu.SMEM)
VMEM = pl.BlockSpec(memory_space=pltpu.VMEM)
NT = (((1,), (1,)), ((), ()))
TN = (((0,), (0,)), ((), ()))
NN = (((1,), (0,)), ((), ()))
MIB = 1024 * 1024


def params(mib=60):
    return pltpu.CompilerParams(vmem_limit_bytes=mib * MIB)


def cost(us):
    return pl.CostEstimate(flops=0, bytes_accessed=int(us * 3e5), transcendentals=0)


def map_copies(maps, table, sem):
    copies, first = [], 0
    for i, m in enumerate(maps):
        copies.append(pltpu.make_async_copy(m, table.at[pl.ds(first, m.shape[0])], sem.at[i]))
        first += m.shape[0]
    return copies


def load_all(copies):
    for copy in copies:
        copy.start()
    for copy in copies:
        copy.wait()


def live_mask(count, rows, width):
    return lax.broadcasted_iota(jnp.int32, (rows, width), 0) < count


def plan_kernel(held, cube, me, table, adapter, owner, idx, wanted):
    for k in range(wanted.shape[0]):
        wanted[k] = -1
    for g in range(owner.shape[0]):
        place = table[adapter[g]]
        who = lax.div(place, held)
        owner[g] = who
        wanted[who] = lax.rem(place, held)
        idx[g] = lax.bitwise_xor(who, me[0]) * held + lax.rem(place, held) if cube else place


def plan(me, table, adapter, held, owners, cube):
    whole = lambda length: jax.ShapeDtypeStruct((length,), jnp.int32)
    segs = adapter.shape[0]
    return pl.pallas_call(
        functools.partial(plan_kernel, held, cube),
        out_shape=[whole(segs), whole(segs), whole(owners)],
        in_specs=[SMEM] * 3,
        out_specs=[SMEM] * 3,
        compiler_params=params(),
        cost_estimate=cost(1),
        name="plan",
    )(me, table, adapter)


def project_kernel(n, per, rows, n_maps, z, idx, count, x, *refs):
    maps, outs, (table, buf, sem) = refs[:n_maps], refs[n_maps : n_maps + n], refs[-3:]
    step = pl.program_id(0)

    @pl.when(step == 0)
    def _():
        load_all(map_copies(maps, table, sem))

    for i in range(per):
        g = step * per + i
        term = lax.dot_general(
            table[idx[g]], x[i * rows : (i + 1) * rows, :], NT, preferred_element_type=jnp.float32
        ).T
        term = jnp.where(live_mask(count[g], *term.shape), term, 0.0)
        buf[pl.ds(pl.multiple_of(g * rows, rows), rows), :] = term

    @pl.when(step == pl.num_programs(0) - 1)
    def _():
        half = outs[0].shape[0]
        for s in range(n):
            start = pl.multiple_of(lax.rem(z[0] + s, n) * 2 * half, 2 * half)
            outs[s][...] = jnp.concatenate(
                [buf[pl.ds(start, half), :], buf[pl.ds(start + half, half), :]], axis=1
            )


def project(z, idx, count, x, maps, n, per, us):
    segs = idx.shape[0]
    rows, width = x.shape[0] // segs, x.shape[1]
    ranks = maps[0].shape[1]
    total = sum(m.shape[0] for m in maps)
    shape = (x.shape[0] // n // 2, 2 * ranks)
    return pl.pallas_call(
        functools.partial(project_kernel, n, per, rows, len(maps)),
        grid=(segs // per,),
        out_shape=[jax.ShapeDtypeStruct(shape, jnp.float32)] * n,
        in_specs=[SMEM] * 3 + [pl.BlockSpec((per * rows, width), lambda i: (i, 0))] + [HBM] * len(maps),
        out_specs=[pl.BlockSpec(shape, lambda i: (0, 0))] * n,
        scratch_shapes=[
            pltpu.VMEM((total, ranks, width), x.dtype),
            pltpu.VMEM((x.shape[0], ranks), jnp.float32),
            pltpu.SemaphoreType.DMA((len(maps),)),
        ],
        compiler_params=params(),
        cost_estimate=cost(us),
        name="project",
    )(z, idx, count, x, *maps)


def cot_copies(n, z, cots, cot, sem):
    key = cots[0].shape[1]
    copies = []
    for s in range(n):
        column = pl.multiple_of(lax.rem(z - s + n, n) * key, key)
        copies.append(pltpu.make_async_copy(cots[s], cot.at[:, pl.ds(column, key)], sem.at[s]))
    return copies


def add_terms(total, owner, terms, x):
    total[owner] += lax.dot_general(terms, x, TN, preferred_element_type=jnp.float32)


def up_sums_kernel(n, owners, rows, scale, z, origin, owner, x_hbm, *refs):
    blocks, outs, (x, raw, buf, total, sem) = refs[:n], refs[n : n + owners], refs[-5:]
    half, ranks = raw.shape[1], raw.shape[2] // 2
    copies = [pltpu.make_async_copy(x_hbm, x, sem.at[n])]
    for s in range(n):
        copies.append(pltpu.make_async_copy(blocks[s], raw.at[lax.rem(z[0] - s + n, n)], sem.at[s]))
    for copy in copies:
        copy.start()
    total[...] = jnp.zeros_like(total)
    for copy in copies:
        copy.wait()
    for j in range(n):
        start = 2 * j * half
        buf[start : start + half, :] = raw[j][:, :ranks]
        buf[start + half : start + 2 * half, :] = raw[j][:, ranks:]
    for g in range(x.shape[0] // rows):
        add_terms(total, owner[g], buf[g * rows : (g + 1) * rows, :], x[g * rows : (g + 1) * rows, :])
    for k, out in enumerate(outs):
        out[...] = (total[lax.bitwise_xor(origin[0], k)] * scale).astype(out.dtype)


def up_sums(z, origin, owner, x, blocks, owners, us):
    segs, n = owner.shape[0], len(blocks)
    rows, width = x.shape[0] // segs, x.shape[1]
    ranks = blocks[0].shape[1] // 2
    shape = (owners, ranks, width)
    return pl.pallas_call(
        functools.partial(up_sums_kernel, n, owners, rows, ADAPTER_SCALE / rows),
        out_shape=[jax.ShapeDtypeStruct(shape[1:], jnp.bfloat16)] * owners,
        in_specs=[SMEM] * 3 + [HBM] * (1 + n),
        out_specs=[VMEM] * owners,
        scratch_shapes=[
            pltpu.VMEM(x.shape, x.dtype),
            pltpu.VMEM((n, *blocks[0].shape), jnp.bfloat16),
            pltpu.VMEM((x.shape[0], ranks), jnp.bfloat16),
            pltpu.VMEM(shape, jnp.float32),
            pltpu.SemaphoreType.DMA((n + 1,)),
        ],
        compiler_params=params(),
        cost_estimate=cost(us),
        name="up_sums",
    )(z, origin, owner, x, *blocks)


def up_copies(maps, size, distances, table, sem):
    key = maps[0].shape[1]
    copies = []
    for i, m in enumerate(maps):
        for k, j in enumerate(distances):
            dst = table.at[pl.ds(i * size, size), pl.ds(k * key, key)]
            copies.append(pltpu.make_async_copy(m.at[pl.ds(j * size, size)], dst, sem.at[i * len(distances) + k]))
    return copies


def pick(place, ranks):
    return pl.ds(pl.multiple_of(place * ranks, ranks), ranks)


def pulled_part_kernel(n, per, rows, ranks, size, n_maps, idx, *refs):
    cots, maps, (out, table, sem) = refs[: n - 1], refs[n - 1 : n - 1 + n_maps], refs[-3:]
    step = pl.program_id(0)

    @pl.when(step == 0)
    def _():
        load_all(up_copies(maps, size, range(n - 1), table, sem))

    for i in range(per):
        x = jnp.concatenate([cot[i * rows : (i + 1) * rows, :] for cot in cots], axis=1)
        out[i * rows : (i + 1) * rows, :] = lax.dot_general(
            x, table[pick(idx[step * per + i], ranks), :], NT, preferred_element_type=jnp.float32
        )


def pulled_part(idx, maps, cots, ranks, size, per, us):
    segs, n = idx.shape[0], len(cots) + 1
    rows, key = cots[0].shape[0] // segs, cots[0].shape[1]
    return pl.pallas_call(
        functools.partial(pulled_part_kernel, n, per, rows, ranks, size, len(maps)),
        grid=(segs // per,),
        out_shape=jax.ShapeDtypeStruct((segs * rows, ranks), jnp.float32),
        in_specs=[SMEM]
        + [pl.BlockSpec((per * rows, key), lambda i: (i, 0))] * (n - 1)
        + [HBM] * len(maps),
        out_specs=pl.BlockSpec((per * rows, ranks), lambda i: (i, 0)),
        scratch_shapes=[
            pltpu.VMEM((size * len(maps), (n - 1) * key), jnp.bfloat16),
            pltpu.SemaphoreType.DMA(((n - 1) * len(maps),)),
        ],
        compiler_params=params(),
        cost_estimate=cost(us),
        name="pulled_part",
    )(idx, *cots, *maps)


def down_sums_kernel(n, per, rows, ranks, size, n_maps, scale, idx, owner, count, x, part, cot, *refs):
    maps, (out, pulled, table, total, sem) = refs[:n_maps], refs[-5:]
    step = pl.program_id(0)

    @pl.when(step == 0)
    def _():
        copies = up_copies(maps, size, [n - 1], table, sem)
        for copy in copies:
            copy.start()
        total[...] = jnp.zeros_like(total)
        for copy in copies:
            copy.wait()

    for i in range(per):
        g = step * per + i
        terms = part[i * rows : (i + 1) * rows, :] + lax.dot_general(
            cot[i * rows : (i + 1) * rows, :], table[pick(idx[g], ranks), :], NT, preferred_element_type=jnp.float32
        )
        terms = jnp.where(live_mask(count[g], *terms.shape), terms, 0.0).astype(pulled.dtype)
        pulled[i * rows : (i + 1) * rows, :] = terms
        add_terms(total, owner[g], terms, x[i * rows : (i + 1) * rows, :])

    @pl.when(step == pl.num_programs(0) - 1)
    def _():
        out[...] = (total[...] * scale).astype(out.dtype)


def down_sums(idx, owner, count, x, part, cot, maps, size, owners, n, per, us):
    segs = owner.shape[0]
    rows, width = x.shape[0] // segs, x.shape[1]
    ranks, key = part.shape[1], cot.shape[1]
    shape = (owners, ranks, width)
    by_rows = lambda columns: pl.BlockSpec((per * rows, columns), lambda i: (i, 0))
    return pl.pallas_call(
        functools.partial(down_sums_kernel, n, per, rows, ranks, size, len(maps), ADAPTER_SCALE / rows),
        grid=(segs // per,),
        out_shape=[
            jax.ShapeDtypeStruct(shape, jnp.bfloat16),
            jax.ShapeDtypeStruct((x.shape[0], ranks), jnp.bfloat16),
        ],
        in_specs=[SMEM] * 3 + [by_rows(width), by_rows(ranks), by_rows(key)] + [HBM] * len(maps),
        out_specs=[pl.BlockSpec(shape, lambda i: (0, 0, 0)), by_rows(ranks)],
        scratch_shapes=[
            pltpu.VMEM((size * len(maps), key), jnp.bfloat16),
            pltpu.VMEM(shape, jnp.float32),
            pltpu.SemaphoreType.DMA((len(maps),)),
        ],
        compiler_params=params(),
        cost_estimate=cost(us),
        name="down_sums",
    )(idx, owner, count, x, part, cot, *maps)


def token_kernel(n, per, rows, n_maps, z, idx, count, weight, pulled, *refs):
    maps, refs = refs[:n_maps], refs[n_maps:]
    cots, (out, table, cot, map_sem, cot_sem) = refs[:n], refs[-5:]
    step = pl.program_id(0)

    @pl.when(step == 0)
    def _():
        load_all(cot_copies(n, z[0], cots, cot, cot_sem) + map_copies(maps, table, map_sem))

    width = weight.shape[1]
    tile = min(512, width)
    counts = [count[step * per + i] for i in range(per)]
    x = cot[pl.ds(pl.multiple_of(step * per * rows, per * rows), per * rows), :]
    for d in range(0, width, tile):
        total = lax.dot_general(x, weight[:, d : d + tile], NN, preferred_element_type=jnp.float32)
        for i in range(per):
            adapter = lax.dot_general(
                pulled[i * rows : (i + 1) * rows, :],
                table[idx[step * per + i], :, d : d + tile],
                NN,
                preferred_element_type=jnp.float32,
            )
            both = total[i * rows : (i + 1) * rows, :] + ADAPTER_SCALE * adapter
            both = jnp.where(live_mask(counts[i], rows, tile), both, 0.0)
            out[i * rows : (i + 1) * rows, d : d + tile] = both.astype(out.dtype)


def token_gradients(z, idx, count, weight, pulled, maps, cots, n, rows, per, after=()):
    segs = idx.shape[0]
    keys, width = weight.shape
    ranks = maps[0].shape[1]
    total = sum(m.shape[0] for m in maps)
    return pl.pallas_call(
        functools.partial(token_kernel, n, per, rows, len(maps)),
        grid=(segs // per,),
        out_shape=jax.ShapeDtypeStruct((segs * rows, width), jnp.bfloat16),
        in_specs=[SMEM] * 3
        + [pl.BlockSpec(weight.shape, lambda i: (0, 0), pipeline_mode=pl.Buffered(1))]
        + [pl.BlockSpec((per * rows, ranks), lambda i: (i, 0))]
        + [HBM] * (len(maps) + n + len(after)),
        out_specs=pl.BlockSpec((per * rows, width), lambda i: (i, 0)),
        scratch_shapes=[
            pltpu.VMEM((total, ranks, width), jnp.bfloat16),
            pltpu.VMEM((segs * rows, keys), jnp.bfloat16),
            pltpu.SemaphoreType.DMA((len(maps),)),
            pltpu.SemaphoreType.DMA((n,)),
        ],
        compiler_params=params(),
        cost_estimate=cost(16),
        name="token_gradient",
    )(z, idx, count, weight, pulled, *maps, *cots, *after)


def told_kernel(row, me, *refs):
    arrays, (out, raw, sem) = refs[:-3], refs[-3:]
    load_all([pltpu.make_async_copy(m.at[pl.ds(row, 16)], raw.at[i], sem.at[i]) for i, m in enumerate(arrays)])
    for i in range(len(arrays)):
        codes = raw[i][:8, :].astype(jnp.float32)
        mine = lax.broadcasted_iota(jnp.int32, codes.shape, 1) == me[0]
        code = jnp.sum(jnp.where(mine, codes, 0.0), axis=1, keepdims=True)
        out[i : i + 1, :] = jnp.broadcast_to(code, (codes.shape[0], out.shape[1]))[:1, :]


def told(me, arrays, row):
    return pl.pallas_call(
        functools.partial(told_kernel, row),
        out_shape=jax.ShapeDtypeStruct((len(arrays), 128), jnp.float32),
        in_specs=[SMEM] + [HBM] * len(arrays),
        out_specs=VMEM,
        scratch_shapes=[
            pltpu.VMEM((len(arrays), 16, arrays[0].shape[1]), arrays[0].dtype),
            pltpu.SemaphoreType.DMA((len(arrays),)),
        ],
        compiler_params=params(),
        cost_estimate=cost(1),
        name="told",
    )(me, *arrays)


def owned_kernel(first, asked, got, out):
    for e in range(out.shape[0]):
        total = jnp.zeros(got.shape[1:], jnp.float32)
        for k in range(got.shape[0]):
            code = asked[pl.ds(lax.bitwise_xor(first[0], k), 1), :1]
            total += jnp.where(code == jnp.float32(e), got[k].astype(jnp.float32), 0.0)
        out[e] = total


def owned(first, asked, got, held, mib):
    peers, ranks, width = got.shape
    per = min(16, ranks)
    return pl.pallas_call(
        owned_kernel,
        grid=(ranks // per,),
        out_shape=jax.ShapeDtypeStruct((held, ranks, width), jnp.float32),
        in_specs=[SMEM, VMEM, pl.BlockSpec((peers, per, width), lambda i: (0, i, 0))],
        out_specs=pl.BlockSpec((held, per, width), lambda i: (0, i, 0)),
        compiler_params=params(mib),
        cost_estimate=cost(2),
        name="owned",
    )(first, asked, got)


def owned_each_kernel(asked, *refs):
    got, out = refs[:-1], refs[-1]
    for e in range(out.shape[0]):
        total = jnp.zeros(got[0].shape, jnp.float32)
        for k, term in enumerate(got):
            total += jnp.where(asked[k : k + 1, :1] == jnp.float32(e), term[...].astype(jnp.float32), 0.0)
        out[e] = total


def owned_each(asked, got, held):
    return pl.pallas_call(
        owned_each_kernel,
        out_shape=jax.ShapeDtypeStruct((held, *got[0].shape), jnp.float32),
        in_specs=[VMEM] * (1 + len(got)),
        out_specs=VMEM,
        compiler_params=params(16),
        cost_estimate=cost(2),
        name="owned_each",
    )(asked, *got)


def gate_kernel(*refs):
    del refs


def gate(*arrays, after=()):
    return pl.pallas_call(
        gate_kernel,
        out_shape=[jax.ShapeDtypeStruct(a.shape, a.dtype) for a in arrays],
        in_specs=[HBM] * (len(arrays) + len(after)),
        out_specs=[HBM] * len(arrays),
        input_output_aliases={i: i for i in range(len(arrays))},
        compiler_params=params(),
        cost_estimate=cost(0),
        name="gate",
    )(*arrays, *after)


def late_kernel(x, *refs):
    out, sem = refs[-2:]
    load_all([pltpu.make_async_copy(x, out, sem)])


def late(x, after):
    return pl.pallas_call(
        late_kernel,
        out_shape=jax.ShapeDtypeStruct(x.shape, x.dtype),
        in_specs=[HBM] * (1 + len(after)),
        out_specs=HBM,
        scratch_shapes=[pltpu.SemaphoreType.DMA(())],
        compiler_params=params(),
        cost_estimate=cost(0),
        name="late",
    )(x, *after)


def ring(x, n):
    return lax.ppermute(x, "tsp", [(i, (i + 1) % n) for i in range(n)])


def flip(x, n, by):
    return lax.ppermute(x, "dp", [(i, i ^ by) for i in range(n)])


def on_device(
    tokens,
    cotangent,
    frozen_key_weight,
    adapter_down_weight,
    adapter_up_weight,
    adapter_place_table,
    segment_adapter,
    segment_live_count,
):
    n_dp = lax.axis_size("dp")
    n = lax.axis_size("tsp")
    me = lax.axis_index("dp").astype(jnp.int32)
    z = lax.axis_index("tsp").astype(jnp.int32)[None]
    held = adapter_down_weight.shape[0]
    segs = segment_adapter.shape[0]
    rows = tokens.shape[0] // segs
    full = segs * rows
    cube = n_dp == 8 and held == 2

    peers = jnp.arange(n_dp, dtype=jnp.int32)
    count = segment_live_count
    ups, downs = adapter_up_weight, adapter_down_weight

    cots = [cotangent, ring(cotangent, n)]
    owner, idx, wanted = plan(me[None], adapter_place_table, segment_adapter, held, n_dp, cube)
    weight = frozen_key_weight.T
    if cube:
        over_x, over_y, weight = gate(flip(downs, n_dp, 2), flip(downs, n_dp, 4), weight)
        ups = late(ups, [over_x, over_y])
    line = [lax.ppermute(ups, "tsp", [(i, (i + s) % n) for i in range(n)]) for s in range(1, n)]
    if cube:
        cots[1], ups, over_x, over_y, *line = gate(cots[1], ups, over_x, over_y, *line)
        corner = [flip(over_x[:1], n_dp, 4), flip(over_y[1:], n_dp, 2)]
    else:
        cots[1], ups, *line = gate(cots[1], ups, *line)

    while len(cots) < n - 1:
        cots.append(ring(cots[-1], n))
    ranks = ups.shape[1]
    size = held * ranks
    info = jnp.zeros((16, ups.shape[2]), ups.dtype).at[0, :n_dp].set(wanted.astype(ups.dtype))
    up_line = jnp.concatenate([u.reshape(size, -1) for u in [ups, *line]] + [info])
    if cube:
        same = [downs, over_x, over_y]
        downs_here = [m for d in same for m in (d, flip(d, n_dp, 1))]
        downs_here += corner + [flip(m, n_dp, 1) for m in corner]
    else:
        downs_here = [lax.all_gather(downs, "dp", axis=0, tiled=True)]
    lowered = project(z, idx, count, tokens, downs_here, n, 4, 4)
    cots[-1], up_line = gate(cots[-1], up_line, after=[lowered[0]])

    cots.append(ring(cots[-1], n))
    if cube:
        same = [up_line] + [flip(up_line, n_dp, k) for k in (2, 4, 6)]
        all_ups = [m for u in same for m in (u, flip(u, n_dp, 1))]
        origin = me[None]
    else:
        all_ups = [lax.all_gather(up_line, "dp", axis=0, tiled=False)[k] for k in range(n_dp)]
        origin = jnp.zeros((1,), jnp.int32)
    asked = told(me[None], all_ups, n * size)
    part = pulled_part(idx, all_ups, cots[:-1], ranks, size, 4, 5)
    cots[-1], *lowered = gate(cots[-1], *lowered, after=[part, asked])

    shift = lambda x, s: lax.ppermute(x, "tsp", [(i, (i + s) % n) for i in range(n)]) if s else x
    parts = [shift(block, s) for s, block in enumerate(lowered)]
    sent, pulled = down_sums(idx, owner, count, tokens, part, cots[-1], all_ups, size, n_dp, n, 4, 7)
    sent, *parts = gate(sent, *parts)
    down_got = lax.all_to_all(sent, "dp", 0, 0, tiled=True)
    lowered = functools.reduce(jnp.add, parts).astype(jnp.bfloat16)
    lowered = [shift(lowered, s) for s in range(n)]
    token_gradient = token_gradients(
        z, idx, count, weight, pulled, downs_here, cots, n, rows, 4, after=lowered[:1]
    )
    lowered[0] = gate(lowered[0], after=[token_gradient])[0]
    got = up_sums(z, origin, owner, cotangent, lowered, n_dp, 2)
    if cube:
        got = [flip(term, n_dp, k) if k else term for k, term in enumerate(got)]
    else:
        got = lax.all_to_all(jnp.stack(got), "dp", 0, 0, tiled=True)
        got = [got[k] for k in range(n_dp)]
    down_grad = owned(origin, asked, down_got, held, 16)
    return token_gradient, down_grad, owned_each(asked, got, held)


def solution(mesh):
    placed = (
        P("dp", "tsp"),
        P("dp", "tsp"),
        P("tsp", None),
        P("dp", None, "tsp"),
        P("dp", None, "tsp"),
        P(),
        P("dp"),
        P("dp"),
    )
    return jax.shard_map(
        on_device,
        mesh=mesh,
        in_specs=placed,
        out_specs=(P("dp", "tsp"), P("dp", None, "tsp"), P("dp", None, "tsp")),
        check_vma=False,
    )
```

```python
import functools

import jax
import jax.numpy as jnp
from jax import lax
from jax.experimental import pallas as pl
from jax.experimental.pallas import tpu as pltpu
from jax.sharding import PartitionSpec as P

ADAPTER_SCALE = 2.0
HBM = pl.BlockSpec(memory_space=pltpu.HBM)
SMEM = pl.BlockSpec(memory_space=pltpu.SMEM)
VMEM = pl.BlockSpec(memory_space=pltpu.VMEM)
NT = (((1,), (1,)), ((), ()))
TN = (((0,), (0,)), ((), ()))
NN = (((1,), (0,)), ((), ()))
MIB = 1024 * 1024


def params(mib=60):
    return pltpu.CompilerParams(vmem_limit_bytes=mib * MIB)


def cost(us):
    return pl.CostEstimate(flops=0, bytes_accessed=int(us * 3e5), transcendentals=0)


def map_copies(maps, table, sem):
    copies, first = [], 0
    for i, m in enumerate(maps):
        copies.append(pltpu.make_async_copy(m, table.at[pl.ds(first, m.shape[0])], sem.at[i]))
        first += m.shape[0]
    return copies


def load_all(copies):
    for copy in copies:
        copy.start()
    for copy in copies:
        copy.wait()


def live_mask(count, rows, width):
    return lax.broadcasted_iota(jnp.int32, (rows, width), 0) < count


def plan_kernel(held, cube, me, table, adapter, owner, idx, wanted):
    for k in range(wanted.shape[0]):
        wanted[k] = -1
    for g in range(owner.shape[0]):
        place = table[adapter[g]]
        who = lax.div(place, held)
        owner[g] = who
        wanted[who] = lax.rem(place, held)
        idx[g] = lax.bitwise_xor(who, me[0]) * held + lax.rem(place, held) if cube else place


def plan(me, table, adapter, held, owners, cube):
    whole = lambda length: jax.ShapeDtypeStruct((length,), jnp.int32)
    segs = adapter.shape[0]
    return pl.pallas_call(
        functools.partial(plan_kernel, held, cube),
        out_shape=[whole(segs), whole(segs), whole(owners)],
        in_specs=[SMEM] * 3,
        out_specs=[SMEM] * 3,
        compiler_params=params(),
        cost_estimate=cost(1),
        name="plan",
    )(me, table, adapter)


def project_kernel(n, per, rows, n_maps, z, idx, count, x, *refs):
    maps, outs, (table, buf, sem) = refs[:n_maps], refs[n_maps : n_maps + n], refs[-3:]
    step = pl.program_id(0)

    @pl.when(step == 0)
    def _():
        load_all(map_copies(maps, table, sem))

    for i in range(per):
        g = step * per + i
        term = lax.dot_general(
            table[idx[g]], x[i * rows : (i + 1) * rows, :], NT, preferred_element_type=jnp.float32
        ).T
        term = jnp.where(live_mask(count[g], *term.shape), term, 0.0)
        buf[pl.ds(pl.multiple_of(g * rows, rows), rows), :] = term

    @pl.when(step == pl.num_programs(0) - 1)
    def _():
        half = outs[0].shape[0]
        for s in range(n):
            start = pl.multiple_of(lax.rem(z[0] + s, n) * 2 * half, 2 * half)
            outs[s][...] = jnp.concatenate(
                [buf[pl.ds(start, half), :], buf[pl.ds(start + half, half), :]], axis=1
            )


def project(z, idx, count, x, maps, n, per, us):
    segs = idx.shape[0]
    rows, width = x.shape[0] // segs, x.shape[1]
    ranks = maps[0].shape[1]
    total = sum(m.shape[0] for m in maps)
    shape = (x.shape[0] // n // 2, 2 * ranks)
    return pl.pallas_call(
        functools.partial(project_kernel, n, per, rows, len(maps)),
        grid=(segs // per,),
        out_shape=[jax.ShapeDtypeStruct(shape, jnp.float32)] * n,
        in_specs=[SMEM] * 3 + [pl.BlockSpec((per * rows, width), lambda i: (i, 0))] + [HBM] * len(maps),
        out_specs=[pl.BlockSpec(shape, lambda i: (0, 0))] * n,
        scratch_shapes=[
            pltpu.VMEM((total, ranks, width), x.dtype),
            pltpu.VMEM((x.shape[0], ranks), jnp.float32),
            pltpu.SemaphoreType.DMA((len(maps),)),
        ],
        compiler_params=params(),
        cost_estimate=cost(us),
        name="project",
    )(z, idx, count, x, *maps)


def cot_copies(n, z, cots, cot, sem):
    key = cots[0].shape[1]
    copies = []
    for s in range(n):
        column = pl.multiple_of(lax.rem(z - s + n, n) * key, key)
        copies.append(pltpu.make_async_copy(cots[s], cot.at[:, pl.ds(column, key)], sem.at[s]))
    return copies


def add_terms(total, owner, terms, x):
    total[owner] += lax.dot_general(terms, x, TN, preferred_element_type=jnp.float32)


def up_sums_kernel(n, owners, rows, scale, z, origin, owner, x_hbm, *refs):
    blocks, outs, (x, raw, buf, total, sem) = refs[:n], refs[n : n + owners], refs[-5:]
    half, ranks = raw.shape[1], raw.shape[2] // 2
    copies = [pltpu.make_async_copy(x_hbm, x, sem.at[n])]
    for s in range(n):
        copies.append(pltpu.make_async_copy(blocks[s], raw.at[lax.rem(z[0] - s + n, n)], sem.at[s]))
    for copy in copies:
        copy.start()
    total[...] = jnp.zeros_like(total)
    for copy in copies:
        copy.wait()
    for j in range(n):
        start = 2 * j * half
        buf[start : start + half, :] = raw[j][:, :ranks]
        buf[start + half : start + 2 * half, :] = raw[j][:, ranks:]
    for g in range(x.shape[0] // rows):
        add_terms(total, owner[g], buf[g * rows : (g + 1) * rows, :], x[g * rows : (g + 1) * rows, :])
    for k, out in enumerate(outs):
        out[...] = (total[lax.bitwise_xor(origin[0], k)] * scale).astype(out.dtype)


def up_sums(z, origin, owner, x, blocks, owners, us):
    segs, n = owner.shape[0], len(blocks)
    rows, width = x.shape[0] // segs, x.shape[1]
    ranks = blocks[0].shape[1] // 2
    shape = (owners, ranks, width)
    return pl.pallas_call(
        functools.partial(up_sums_kernel, n, owners, rows, ADAPTER_SCALE / rows),
        out_shape=[jax.ShapeDtypeStruct(shape[1:], jnp.bfloat16)] * owners,
        in_specs=[SMEM] * 3 + [HBM] * (1 + n),
        out_specs=[VMEM] * owners,
        scratch_shapes=[
            pltpu.VMEM(x.shape, x.dtype),
            pltpu.VMEM((n, *blocks[0].shape), jnp.bfloat16),
            pltpu.VMEM((x.shape[0], ranks), jnp.bfloat16),
            pltpu.VMEM(shape, jnp.float32),
            pltpu.SemaphoreType.DMA((n + 1,)),
        ],
        compiler_params=params(),
        cost_estimate=cost(us),
        name="up_sums",
    )(z, origin, owner, x, *blocks)


def up_copies(maps, size, distances, table, sem):
    key = maps[0].shape[1]
    copies = []
    for i, m in enumerate(maps):
        for k, j in enumerate(distances):
            dst = table.at[pl.ds(i * size, size), pl.ds(k * key, key)]
            copies.append(pltpu.make_async_copy(m.at[pl.ds(j * size, size)], dst, sem.at[i * len(distances) + k]))
    return copies


def pick(place, ranks):
    return pl.ds(pl.multiple_of(place * ranks, ranks), ranks)


def pulled_part_kernel(n, per, rows, ranks, size, n_maps, idx, *refs):
    cots, maps, (out, table, sem) = refs[: n - 1], refs[n - 1 : n - 1 + n_maps], refs[-3:]
    step = pl.program_id(0)

    @pl.when(step == 0)
    def _():
        load_all(up_copies(maps, size, range(n - 1), table, sem))

    for i in range(per):
        x = jnp.concatenate([cot[i * rows : (i + 1) * rows, :] for cot in cots], axis=1)
        out[i * rows : (i + 1) * rows, :] = lax.dot_general(
            x, table[pick(idx[step * per + i], ranks), :], NT, preferred_element_type=jnp.float32
        )


def pulled_part(idx, maps, cots, ranks, size, per, us):
    segs, n = idx.shape[0], len(cots) + 1
    rows, key = cots[0].shape[0] // segs, cots[0].shape[1]
    return pl.pallas_call(
        functools.partial(pulled_part_kernel, n, per, rows, ranks, size, len(maps)),
        grid=(segs // per,),
        out_shape=jax.ShapeDtypeStruct((segs * rows, ranks), jnp.float32),
        in_specs=[SMEM]
        + [pl.BlockSpec((per * rows, key), lambda i: (i, 0))] * (n - 1)
        + [HBM] * len(maps),
        out_specs=pl.BlockSpec((per * rows, ranks), lambda i: (i, 0)),
        scratch_shapes=[
            pltpu.VMEM((size * len(maps), (n - 1) * key), jnp.bfloat16),
            pltpu.SemaphoreType.DMA(((n - 1) * len(maps),)),
        ],
        compiler_params=params(),
        cost_estimate=cost(us),
        name="pulled_part",
    )(idx, *cots, *maps)


def down_sums_kernel(n, per, rows, ranks, size, n_maps, scale, idx, owner, count, x, part, cot, *refs):
    maps, (out, pulled, table, total, sem) = refs[:n_maps], refs[-5:]
    step = pl.program_id(0)

    @pl.when(step == 0)
    def _():
        copies = up_copies(maps, size, [n - 1], table, sem)
        for copy in copies:
            copy.start()
        total[...] = jnp.zeros_like(total)
        for copy in copies:
            copy.wait()

    for i in range(per):
        g = step * per + i
        terms = part[i * rows : (i + 1) * rows, :] + lax.dot_general(
            cot[i * rows : (i + 1) * rows, :], table[pick(idx[g], ranks), :], NT, preferred_element_type=jnp.float32
        )
        terms = jnp.where(live_mask(count[g], *terms.shape), terms, 0.0).astype(pulled.dtype)
        pulled[i * rows : (i + 1) * rows, :] = terms
        add_terms(total, owner[g], terms, x[i * rows : (i + 1) * rows, :])

    @pl.when(step == pl.num_programs(0) - 1)
    def _():
        out[...] = (total[...] * scale).astype(out.dtype)


def down_sums(idx, owner, count, x, part, cot, maps, size, owners, n, per, us):
    segs = owner.shape[0]
    rows, width = x.shape[0] // segs, x.shape[1]
    ranks, key = part.shape[1], cot.shape[1]
    shape = (owners, ranks, width)
    by_rows = lambda columns: pl.BlockSpec((per * rows, columns), lambda i: (i, 0))
    return pl.pallas_call(
        functools.partial(down_sums_kernel, n, per, rows, ranks, size, len(maps), ADAPTER_SCALE / rows),
        grid=(segs // per,),
        out_shape=[
            jax.ShapeDtypeStruct(shape, jnp.bfloat16),
            jax.ShapeDtypeStruct((x.shape[0], ranks), jnp.bfloat16),
        ],
        in_specs=[SMEM] * 3 + [by_rows(width), by_rows(ranks), by_rows(key)] + [HBM] * len(maps),
        out_specs=[pl.BlockSpec(shape, lambda i: (0, 0, 0)), by_rows(ranks)],
        scratch_shapes=[
            pltpu.VMEM((size * len(maps), key), jnp.bfloat16),
            pltpu.VMEM(shape, jnp.float32),
            pltpu.SemaphoreType.DMA((len(maps),)),
        ],
        compiler_params=params(),
        cost_estimate=cost(us),
        name="down_sums",
    )(idx, owner, count, x, part, cot, *maps)


def token_kernel(n, per, rows, n_maps, z, idx, count, weight, pulled, *refs):
    maps, refs = refs[:n_maps], refs[n_maps:]
    cots, (out, table, cot, map_sem, cot_sem) = refs[:n], refs[-5:]
    step = pl.program_id(0)

    @pl.when(step == 0)
    def _():
        load_all(cot_copies(n, z[0], cots, cot, cot_sem) + map_copies(maps, table, map_sem))

    width = weight.shape[1]
    tile = min(512, width)
    counts = [count[step * per + i] for i in range(per)]
    x = cot[pl.ds(pl.multiple_of(step * per * rows, per * rows), per * rows), :]
    for d in range(0, width, tile):
        total = lax.dot_general(x, weight[:, d : d + tile], NN, preferred_element_type=jnp.float32)
        for i in range(per):
            adapter = lax.dot_general(
                pulled[i * rows : (i + 1) * rows, :],
                table[idx[step * per + i], :, d : d + tile],
                NN,
                preferred_element_type=jnp.float32,
            )
            both = total[i * rows : (i + 1) * rows, :] + ADAPTER_SCALE * adapter
            both = jnp.where(live_mask(counts[i], rows, tile), both, 0.0)
            out[i * rows : (i + 1) * rows, d : d + tile] = both.astype(out.dtype)


def token_gradients(z, idx, count, weight, pulled, maps, cots, n, rows, per, after=()):
    segs = idx.shape[0]
    keys, width = weight.shape
    ranks = maps[0].shape[1]
    total = sum(m.shape[0] for m in maps)
    return pl.pallas_call(
        functools.partial(token_kernel, n, per, rows, len(maps)),
        grid=(segs // per,),
        out_shape=jax.ShapeDtypeStruct((segs * rows, width), jnp.bfloat16),
        in_specs=[SMEM] * 3
        + [pl.BlockSpec(weight.shape, lambda i: (0, 0), pipeline_mode=pl.Buffered(1))]
        + [pl.BlockSpec((per * rows, ranks), lambda i: (i, 0))]
        + [HBM] * (len(maps) + n + len(after)),
        out_specs=pl.BlockSpec((per * rows, width), lambda i: (i, 0)),
        scratch_shapes=[
            pltpu.VMEM((total, ranks, width), jnp.bfloat16),
            pltpu.VMEM((segs * rows, keys), jnp.bfloat16),
            pltpu.SemaphoreType.DMA((len(maps),)),
            pltpu.SemaphoreType.DMA((n,)),
        ],
        compiler_params=params(),
        cost_estimate=cost(16),
        name="token_gradient",
    )(z, idx, count, weight, pulled, *maps, *cots, *after)


def told_kernel(row, me, *refs):
    arrays, (out, raw, sem) = refs[:-3], refs[-3:]
    load_all([pltpu.make_async_copy(m.at[pl.ds(row, 16)], raw.at[i], sem.at[i]) for i, m in enumerate(arrays)])
    for i in range(len(arrays)):
        codes = raw[i][:8, :].astype(jnp.float32)
        mine = lax.broadcasted_iota(jnp.int32, codes.shape, 1) == me[0]
        code = jnp.sum(jnp.where(mine, codes, 0.0), axis=1, keepdims=True)
        out[i : i + 1, :] = jnp.broadcast_to(code, (codes.shape[0], out.shape[1]))[:1, :]


def told(me, arrays, row):
    return pl.pallas_call(
        functools.partial(told_kernel, row),
        out_shape=jax.ShapeDtypeStruct((len(arrays), 128), jnp.float32),
        in_specs=[SMEM] + [HBM] * len(arrays),
        out_specs=VMEM,
        scratch_shapes=[
            pltpu.VMEM((len(arrays), 16, arrays[0].shape[1]), arrays[0].dtype),
            pltpu.SemaphoreType.DMA((len(arrays),)),
        ],
        compiler_params=params(),
        cost_estimate=cost(1),
        name="told",
    )(me, *arrays)


def owned_kernel(first, asked, got, out):
    for e in range(out.shape[0]):
        total = jnp.zeros(got.shape[1:], jnp.float32)
        for k in range(got.shape[0]):
            code = asked[pl.ds(lax.bitwise_xor(first[0], k), 1), :1]
            total += jnp.where(code == jnp.float32(e), got[k].astype(jnp.float32), 0.0)
        out[e] = total


def owned(first, asked, got, held, mib):
    peers, ranks, width = got.shape
    per = min(16, ranks)
    return pl.pallas_call(
        owned_kernel,
        grid=(ranks // per,),
        out_shape=jax.ShapeDtypeStruct((held, ranks, width), jnp.float32),
        in_specs=[SMEM, VMEM, pl.BlockSpec((peers, per, width), lambda i: (0, i, 0))],
        out_specs=pl.BlockSpec((held, per, width), lambda i: (0, i, 0)),
        compiler_params=params(mib),
        cost_estimate=cost(2),
        name="owned",
    )(first, asked, got)


def owned_each_kernel(asked, *refs):
    got, out = refs[:-2], refs[-1]
    for e in range(out.shape[0]):
        total = jnp.zeros(got[0].shape, jnp.float32)
        for k, term in enumerate(got):
            total += jnp.where(asked[k : k + 1, :1] == jnp.float32(e), term[...].astype(jnp.float32), 0.0)
        out[e] = total


def owned_each(asked, got, held, after):
    return pl.pallas_call(
        owned_each_kernel,
        out_shape=jax.ShapeDtypeStruct((held, *got[0].shape), jnp.float32),
        in_specs=[VMEM] * (1 + len(got)) + [HBM],
        out_specs=VMEM,
        compiler_params=params(),
        cost_estimate=cost(2),
        name="owned_each",
    )(asked, *got, after)


def gate_kernel(*refs):
    del refs


def gate(*arrays, after=()):
    return pl.pallas_call(
        gate_kernel,
        out_shape=[jax.ShapeDtypeStruct(a.shape, a.dtype) for a in arrays],
        in_specs=[HBM] * (len(arrays) + len(after)),
        out_specs=[HBM] * len(arrays),
        input_output_aliases={i: i for i in range(len(arrays))},
        compiler_params=params(),
        cost_estimate=cost(0),
        name="gate",
    )(*arrays, *after)


def late_kernel(x, *refs):
    out, sem = refs[-2:]
    load_all([pltpu.make_async_copy(x, out, sem)])


def late(x, after):
    return pl.pallas_call(
        late_kernel,
        out_shape=jax.ShapeDtypeStruct(x.shape, x.dtype),
        in_specs=[HBM] * (1 + len(after)),
        out_specs=HBM,
        scratch_shapes=[pltpu.SemaphoreType.DMA(())],
        compiler_params=params(),
        cost_estimate=cost(0),
        name="late",
    )(x, *after)


def ring(x, n):
    return lax.ppermute(x, "tsp", [(i, (i + 1) % n) for i in range(n)])


def flip(x, n, by):
    return lax.ppermute(x, "dp", [(i, i ^ by) for i in range(n)])


def on_device(
    tokens,
    cotangent,
    frozen_key_weight,
    adapter_down_weight,
    adapter_up_weight,
    adapter_place_table,
    segment_adapter,
    segment_live_count,
):
    n_dp = lax.axis_size("dp")
    n = lax.axis_size("tsp")
    me = lax.axis_index("dp").astype(jnp.int32)
    z = lax.axis_index("tsp").astype(jnp.int32)[None]
    held = adapter_down_weight.shape[0]
    segs = segment_adapter.shape[0]
    rows = tokens.shape[0] // segs
    full = segs * rows
    cube = n_dp == 8 and held == 2

    peers = jnp.arange(n_dp, dtype=jnp.int32)
    count = segment_live_count
    ups, downs = adapter_up_weight, adapter_down_weight

    cots = [cotangent, ring(cotangent, n)]
    owner, idx, wanted = plan(me[None], adapter_place_table, segment_adapter, held, n_dp, cube)
    weight = frozen_key_weight.T
    if cube:
        over_x, over_y, weight = gate(flip(downs, n_dp, 2), flip(downs, n_dp, 4), weight)
        ups = late(ups, [over_x, over_y])
    line = [lax.ppermute(ups, "tsp", [(i, (i + s) % n) for i in range(n)]) for s in range(1, n)]
    if cube:
        cots[1], ups, over_x, over_y, *line = gate(cots[1], ups, over_x, over_y, *line)
        corner = [flip(over_x[:1], n_dp, 4), flip(over_y[1:], n_dp, 2)]
    else:
        cots[1], ups, *line = gate(cots[1], ups, *line)

    while len(cots) < n - 1:
        cots.append(ring(cots[-1], n))
    ranks = ups.shape[1]
    size = held * ranks
    info = jnp.zeros((16, ups.shape[2]), ups.dtype).at[0, :n_dp].set(wanted.astype(ups.dtype))
    up_line = jnp.concatenate([u.reshape(size, -1) for u in [ups, *line]] + [info])
    if cube:
        same = [downs, over_x, over_y]
        downs_here = [m for d in same for m in (d, flip(d, n_dp, 1))]
        downs_here += corner + [flip(m, n_dp, 1) for m in corner]
    else:
        downs_here = [lax.all_gather(downs, "dp", axis=0, tiled=True)]
    lowered = project(z, idx, count, tokens, downs_here, n, 4, 4)
    cots[-1], up_line = gate(cots[-1], up_line, after=[lowered[0]])

    cots.append(ring(cots[-1], n))
    if cube:
        same = [up_line] + [flip(up_line, n_dp, k) for k in (2, 4, 6)]
        all_ups = [m for u in same for m in (u, flip(u, n_dp, 1))]
        origin = me[None]
    else:
        all_ups = [lax.all_gather(up_line, "dp", axis=0, tiled=False)[k] for k in range(n_dp)]
        origin = jnp.zeros((1,), jnp.int32)
    asked = told(me[None], all_ups, n * size)
    part = pulled_part(idx, all_ups, cots[:-1], ranks, size, 4, 5)
    cots[-1], *lowered = gate(cots[-1], *lowered, after=[part, asked])

    shift = lambda x, s: lax.ppermute(x, "tsp", [(i, (i + s) % n) for i in range(n)]) if s else x
    parts = [shift(block, s) for s, block in enumerate(lowered)]
    sent, pulled = down_sums(idx, owner, count, tokens, part, cots[-1], all_ups, size, n_dp, n, 4, 7)
    sent, *parts = gate(sent, *parts)
    down_got = lax.all_to_all(sent, "dp", 0, 0, tiled=True)
    lowered = functools.reduce(jnp.add, parts).astype(jnp.bfloat16)
    lowered = [shift(lowered, s) for s in range(n)]
    token_gradient = token_gradients(
        z, idx, count, weight, pulled, downs_here, cots, n, rows, 4, after=lowered[:1]
    )
    lowered[0] = gate(lowered[0], after=[token_gradient])[0]
    got = up_sums(z, origin, owner, cotangent, lowered, n_dp, 2)
    if cube:
        got = [flip(term, n_dp, k) if k else term for k, term in enumerate(got)]
    else:
        got = lax.all_to_all(jnp.stack(got), "dp", 0, 0, tiled=True)
        got = [got[k] for k in range(n_dp)]
    down_grad = owned(origin, asked, down_got, held, 16)
    return token_gradient, down_grad, owned_each(asked, got, held, down_grad)


def solution(mesh):
    placed = (
        P("dp", "tsp"),
        P("dp", "tsp"),
        P("tsp", None),
        P("dp", None, "tsp"),
        P("dp", None, "tsp"),
        P(),
        P("dp"),
        P("dp"),
    )
    return jax.shard_map(
        on_device,
        mesh=mesh,
        in_specs=placed,
        out_specs=(P("dp", "tsp"), P("dp", None, "tsp"), P("dp", None, "tsp")),
        check_vma=False,
    )
```

```python
import functools

import jax
import jax.numpy as jnp
from jax import lax
from jax.experimental import pallas as pl
from jax.experimental.pallas import tpu as pltpu
from jax.sharding import PartitionSpec as P

ADAPTER_SCALE = 2.0
HBM = pl.BlockSpec(memory_space=pltpu.HBM)
SMEM = pl.BlockSpec(memory_space=pltpu.SMEM)
VMEM = pl.BlockSpec(memory_space=pltpu.VMEM)
NT = (((1,), (1,)), ((), ()))
TN = (((0,), (0,)), ((), ()))
NN = (((1,), (0,)), ((), ()))
MIB = 1024 * 1024


def params(mib=60):
    return pltpu.CompilerParams(vmem_limit_bytes=mib * MIB)


def cost(us):
    return pl.CostEstimate(flops=0, bytes_accessed=int(us * 3e5), transcendentals=0)


def map_copies(maps, table, sem):
    copies, first = [], 0
    for i, m in enumerate(maps):
        copies.append(pltpu.make_async_copy(m, table.at[pl.ds(first, m.shape[0])], sem.at[i]))
        first += m.shape[0]
    return copies


def load_all(copies):
    for copy in copies:
        copy.start()
    for copy in copies:
        copy.wait()


def live_mask(count, rows, width):
    return lax.broadcasted_iota(jnp.int32, (rows, width), 0) < count


def plan_kernel(held, cube, me, table, adapter, owner, idx, wanted):
    for k in range(wanted.shape[0]):
        wanted[k] = -1
    for g in range(owner.shape[0]):
        place = table[adapter[g]]
        who = lax.div(place, held)
        owner[g] = who
        wanted[who] = lax.rem(place, held)
        idx[g] = lax.bitwise_xor(who, me[0]) * held + lax.rem(place, held) if cube else place


def plan(me, table, adapter, held, owners, cube):
    whole = lambda length: jax.ShapeDtypeStruct((length,), jnp.int32)
    segs = adapter.shape[0]
    return pl.pallas_call(
        functools.partial(plan_kernel, held, cube),
        out_shape=[whole(segs), whole(segs), whole(owners)],
        in_specs=[SMEM] * 3,
        out_specs=[SMEM] * 3,
        compiler_params=params(),
        cost_estimate=cost(1),
        name="plan",
    )(me, table, adapter)


def project_kernel(n, per, rows, n_maps, z, idx, count, x, *refs):
    maps, outs, (table, buf, sem) = refs[:n_maps], refs[n_maps : n_maps + n], refs[-3:]
    step = pl.program_id(0)

    @pl.when(step == 0)
    def _():
        load_all(map_copies(maps, table, sem))

    for i in range(per):
        g = step * per + i
        term = lax.dot_general(
            table[idx[g]], x[i * rows : (i + 1) * rows, :], NT, preferred_element_type=jnp.float32
        ).T
        term = jnp.where(live_mask(count[g], *term.shape), term, 0.0)
        buf[pl.ds(pl.multiple_of(g * rows, rows), rows), :] = term

    @pl.when(step == pl.num_programs(0) - 1)
    def _():
        half = outs[0].shape[0]
        for s in range(n):
            start = pl.multiple_of(lax.rem(z[0] + s, n) * 2 * half, 2 * half)
            outs[s][...] = jnp.concatenate(
                [buf[pl.ds(start, half), :], buf[pl.ds(start + half, half), :]], axis=1
            )


def project(z, idx, count, x, maps, n, per, us):
    segs = idx.shape[0]
    rows, width = x.shape[0] // segs, x.shape[1]
    ranks = maps[0].shape[1]
    total = sum(m.shape[0] for m in maps)
    shape = (x.shape[0] // n // 2, 2 * ranks)
    return pl.pallas_call(
        functools.partial(project_kernel, n, per, rows, len(maps)),
        grid=(segs // per,),
        out_shape=[jax.ShapeDtypeStruct(shape, jnp.float32)] * n,
        in_specs=[SMEM] * 3 + [pl.BlockSpec((per * rows, width), lambda i: (i, 0))] + [HBM] * len(maps),
        out_specs=[pl.BlockSpec(shape, lambda i: (0, 0))] * n,
        scratch_shapes=[
            pltpu.VMEM((total, ranks, width), x.dtype),
            pltpu.VMEM((x.shape[0], ranks), jnp.float32),
            pltpu.SemaphoreType.DMA((len(maps),)),
        ],
        compiler_params=params(),
        cost_estimate=cost(us),
        name="project",
    )(z, idx, count, x, *maps)


def cot_copies(n, z, cots, cot, first, size, sem, at):
    key = cots[0].shape[1]
    copies = []
    for s in range(n):
        column = pl.multiple_of(lax.rem(z - s + n, n) * key, key)
        dst = cot.at[pl.ds(first, size), pl.ds(column, key)]
        copies.append(pltpu.make_async_copy(cots[s].at[pl.ds(first, size)], dst, sem.at[at + s]))
    return copies


def add_terms(total, owner, terms, x):
    total[owner] += lax.dot_general(terms, x, TN, preferred_element_type=jnp.float32)


def up_sums_kernel(n, owners, rows, scale, z, origin, owner, x_hbm, *refs):
    blocks, outs, (x, raw, buf, total, sem) = refs[:n], refs[n : n + owners], refs[-5:]
    half, ranks = raw.shape[1], raw.shape[2] // 2
    copies = [pltpu.make_async_copy(x_hbm, x, sem.at[n])]
    for s in range(n):
        copies.append(pltpu.make_async_copy(blocks[s], raw.at[lax.rem(z[0] - s + n, n)], sem.at[s]))
    for copy in copies:
        copy.start()
    total[...] = jnp.zeros_like(total)
    for copy in copies:
        copy.wait()
    for j in range(n):
        start = 2 * j * half
        buf[start : start + half, :] = raw[j][:, :ranks]
        buf[start + half : start + 2 * half, :] = raw[j][:, ranks:]
    for g in range(x.shape[0] // rows):
        add_terms(total, owner[g], buf[g * rows : (g + 1) * rows, :], x[g * rows : (g + 1) * rows, :])
    for k, out in enumerate(outs):
        out[...] = (total[lax.bitwise_xor(origin[0], k)] * scale).astype(out.dtype)


def up_sums(z, origin, owner, x, blocks, owners, us):
    segs, n = owner.shape[0], len(blocks)
    rows, width = x.shape[0] // segs, x.shape[1]
    ranks = blocks[0].shape[1] // 2
    shape = (owners, ranks, width)
    return pl.pallas_call(
        functools.partial(up_sums_kernel, n, owners, rows, ADAPTER_SCALE / rows),
        out_shape=[jax.ShapeDtypeStruct(shape[1:], jnp.bfloat16)] * owners,
        in_specs=[SMEM] * 3 + [HBM] * (1 + n),
        out_specs=[VMEM] * owners,
        scratch_shapes=[
            pltpu.VMEM(x.shape, x.dtype),
            pltpu.VMEM((n, *blocks[0].shape), jnp.bfloat16),
            pltpu.VMEM((x.shape[0], ranks), jnp.bfloat16),
            pltpu.VMEM(shape, jnp.float32),
            pltpu.SemaphoreType.DMA((n + 1,)),
        ],
        compiler_params=params(),
        cost_estimate=cost(us),
        name="up_sums",
    )(z, origin, owner, x, *blocks)


def up_copies(maps, size, distances, table, sem):
    key = maps[0].shape[1]
    copies = []
    for i, m in enumerate(maps):
        for k, j in enumerate(distances):
            dst = table.at[pl.ds(i * size, size), pl.ds(k * key, key)]
            copies.append(pltpu.make_async_copy(m.at[pl.ds(j * size, size)], dst, sem.at[i * len(distances) + k]))
    return copies


def pick(place, ranks):
    return pl.ds(pl.multiple_of(place * ranks, ranks), ranks)


def pulled_part_kernel(n, per, rows, ranks, size, n_maps, idx, *refs):
    cots, maps, (out, table, sem) = refs[: n - 1], refs[n - 1 : n - 1 + n_maps], refs[-3:]
    step = pl.program_id(0)

    @pl.when(step == 0)
    def _():
        load_all(up_copies(maps, size, range(n - 1), table, sem))

    for i in range(per):
        x = jnp.concatenate([cot[i * rows : (i + 1) * rows, :] for cot in cots], axis=1)
        out[i * rows : (i + 1) * rows, :] = lax.dot_general(
            x, table[pick(idx[step * per + i], ranks), :], NT, preferred_element_type=jnp.float32
        )


def pulled_part(idx, maps, cots, ranks, size, per, us):
    segs, n = idx.shape[0], len(cots) + 1
    rows, key = cots[0].shape[0] // segs, cots[0].shape[1]
    return pl.pallas_call(
        functools.partial(pulled_part_kernel, n, per, rows, ranks, size, len(maps)),
        grid=(segs // per,),
        out_shape=jax.ShapeDtypeStruct((segs * rows, ranks), jnp.float32),
        in_specs=[SMEM]
        + [pl.BlockSpec((per * rows, key), lambda i: (i, 0))] * (n - 1)
        + [HBM] * len(maps),
        out_specs=pl.BlockSpec((per * rows, ranks), lambda i: (i, 0)),
        scratch_shapes=[
            pltpu.VMEM((size * len(maps), (n - 1) * key), jnp.bfloat16),
            pltpu.SemaphoreType.DMA(((n - 1) * len(maps),)),
        ],
        compiler_params=params(),
        cost_estimate=cost(us),
        name="pulled_part",
    )(idx, *cots, *maps)


def down_sums_kernel(n, per, rows, ranks, size, n_maps, scale, idx, owner, count, x, part, cot, *refs):
    maps, (out, pulled, table, total, sem) = refs[:n_maps], refs[-5:]
    step = pl.program_id(0)

    @pl.when(step == 0)
    def _():
        copies = up_copies(maps, size, [n - 1], table, sem)
        for copy in copies:
            copy.start()
        total[...] = jnp.zeros_like(total)
        for copy in copies:
            copy.wait()

    for i in range(per):
        g = step * per + i
        terms = part[i * rows : (i + 1) * rows, :] + lax.dot_general(
            cot[i * rows : (i + 1) * rows, :], table[pick(idx[g], ranks), :], NT, preferred_element_type=jnp.float32
        )
        terms = jnp.where(live_mask(count[g], *terms.shape), terms, 0.0).astype(pulled.dtype)
        pulled[i * rows : (i + 1) * rows, :] = terms
        add_terms(total, owner[g], terms, x[i * rows : (i + 1) * rows, :])

    @pl.when(step == pl.num_programs(0) - 1)
    def _():
        out[...] = (total[...] * scale).astype(out.dtype)


def down_sums(idx, owner, count, x, part, cot, maps, size, owners, n, per, us):
    segs = owner.shape[0]
    rows, width = x.shape[0] // segs, x.shape[1]
    ranks, key = part.shape[1], cot.shape[1]
    shape = (owners, ranks, width)
    by_rows = lambda columns: pl.BlockSpec((per * rows, columns), lambda i: (i, 0))
    return pl.pallas_call(
        functools.partial(down_sums_kernel, n, per, rows, ranks, size, len(maps), ADAPTER_SCALE / rows),
        grid=(segs // per,),
        out_shape=[
            jax.ShapeDtypeStruct(shape, jnp.bfloat16),
            jax.ShapeDtypeStruct((x.shape[0], ranks), jnp.bfloat16),
        ],
        in_specs=[SMEM] * 3 + [by_rows(width), by_rows(ranks), by_rows(key)] + [HBM] * len(maps),
        out_specs=[pl.BlockSpec(shape, lambda i: (0, 0, 0)), by_rows(ranks)],
        scratch_shapes=[
            pltpu.VMEM((size * len(maps), key), jnp.bfloat16),
            pltpu.VMEM(shape, jnp.float32),
            pltpu.SemaphoreType.DMA((len(maps),)),
        ],
        compiler_params=params(),
        cost_estimate=cost(us),
        name="down_sums",
    )(idx, owner, count, x, part, cot, *maps)


def token_kernel(n, per, rows, n_maps, z, idx, count, weight, pulled, *refs):
    maps, refs = refs[:n_maps], refs[n_maps:]
    cots, (out, table, cot, map_sem, cot_sem) = refs[:n], refs[-5:]
    step = pl.program_id(0)
    block = per * rows

    @pl.when(step == 0)
    def _():
        for k in range(cot.shape[0] // block):
            for copy in cot_copies(n, z[0], cots, cot, k * block, block, cot_sem, k * n):
                copy.start()
        for copy in map_copies(maps, table, map_sem):
            copy.start()

    begin = pl.multiple_of(step * block, block)
    for copy in cot_copies(n, z[0], cots, cot, begin, block, cot_sem, step * n):
        copy.wait()
    width = weight.shape[1]
    tile = min(512, width)
    counts = [count[step * per + i] for i in range(per)]
    x = cot[pl.ds(begin, block), :]
    for d in range(0, width, tile):
        total = lax.dot_general(x, weight[:, d : d + tile], NN, preferred_element_type=jnp.float32)
        if d == 0:

            @pl.when(step == 0)
            def _():
                for copy in map_copies(maps, table, map_sem):
                    copy.wait()

        for i in range(per):
            adapter = lax.dot_general(
                pulled[i * rows : (i + 1) * rows, :],
                table[idx[step * per + i], :, d : d + tile],
                NN,
                preferred_element_type=jnp.float32,
            )
            both = total[i * rows : (i + 1) * rows, :] + ADAPTER_SCALE * adapter
            both = jnp.where(live_mask(counts[i], rows, tile), both, 0.0)
            out[i * rows : (i + 1) * rows, d : d + tile] = both.astype(out.dtype)


def token_gradients(z, idx, count, weight, pulled, maps, cots, n, rows, per, after=()):
    segs = idx.shape[0]
    keys, width = weight.shape
    ranks = maps[0].shape[1]
    total = sum(m.shape[0] for m in maps)
    return pl.pallas_call(
        functools.partial(token_kernel, n, per, rows, len(maps)),
        grid=(segs // per,),
        out_shape=jax.ShapeDtypeStruct((segs * rows, width), jnp.bfloat16),
        in_specs=[SMEM] * 3
        + [pl.BlockSpec(weight.shape, lambda i: (0, 0), pipeline_mode=pl.Buffered(1))]
        + [pl.BlockSpec((per * rows, ranks), lambda i: (i, 0))]
        + [HBM] * (len(maps) + n + len(after)),
        out_specs=pl.BlockSpec((per * rows, width), lambda i: (i, 0)),
        scratch_shapes=[
            pltpu.VMEM((total, ranks, width), jnp.bfloat16),
            pltpu.VMEM((segs * rows, keys), jnp.bfloat16),
            pltpu.SemaphoreType.DMA((len(maps),)),
            pltpu.SemaphoreType.DMA((n * segs // per,)),
        ],
        compiler_params=params(),
        cost_estimate=cost(16),
        name="token_gradient",
    )(z, idx, count, weight, pulled, *maps, *cots, *after)


def told_kernel(row, me, *refs):
    arrays, (out, raw, sem) = refs[:-3], refs[-3:]
    load_all([pltpu.make_async_copy(m.at[pl.ds(row, 16)], raw.at[i], sem.at[i]) for i, m in enumerate(arrays)])
    for i in range(len(arrays)):
        codes = raw[i][:8, :].astype(jnp.float32)
        mine = lax.broadcasted_iota(jnp.int32, codes.shape, 1) == me[0]
        code = jnp.sum(jnp.where(mine, codes, 0.0), axis=1, keepdims=True)
        out[i : i + 1, :] = jnp.broadcast_to(code, (codes.shape[0], out.shape[1]))[:1, :]


def told(me, arrays, row):
    return pl.pallas_call(
        functools.partial(told_kernel, row),
        out_shape=jax.ShapeDtypeStruct((len(arrays), 128), jnp.float32),
        in_specs=[SMEM] + [HBM] * len(arrays),
        out_specs=VMEM,
        scratch_shapes=[
            pltpu.VMEM((len(arrays), 16, arrays[0].shape[1]), arrays[0].dtype),
            pltpu.SemaphoreType.DMA((len(arrays),)),
        ],
        compiler_params=params(),
        cost_estimate=cost(1),
        name="told",
    )(me, *arrays)


def owned_kernel(first, asked, got, out):
    for e in range(out.shape[0]):
        total = jnp.zeros(got.shape[1:], jnp.float32)
        for k in range(got.shape[0]):
            code = asked[pl.ds(lax.bitwise_xor(first[0], k), 1), :1]
            total += jnp.where(code == jnp.float32(e), got[k].astype(jnp.float32), 0.0)
        out[e] = total


def owned(first, asked, got, held, mib):
    peers, ranks, width = got.shape
    per = min(16, ranks)
    return pl.pallas_call(
        owned_kernel,
        grid=(ranks // per,),
        out_shape=jax.ShapeDtypeStruct((held, ranks, width), jnp.float32),
        in_specs=[SMEM, VMEM, pl.BlockSpec((peers, per, width), lambda i: (0, i, 0))],
        out_specs=pl.BlockSpec((held, per, width), lambda i: (0, i, 0)),
        compiler_params=params(mib),
        cost_estimate=cost(2),
        name="owned",
    )(first, asked, got)


def owned_each_kernel(asked, *refs):
    got, out = refs[:-2], refs[-1]
    for e in range(out.shape[0]):
        total = jnp.zeros(got[0].shape, jnp.float32)
        for k, term in enumerate(got):
            total += jnp.where(asked[k : k + 1, :1] == jnp.float32(e), term[...].astype(jnp.float32), 0.0)
        out[e] = total


def owned_each(asked, got, held, after):
    return pl.pallas_call(
        owned_each_kernel,
        out_shape=jax.ShapeDtypeStruct((held, *got[0].shape), jnp.float32),
        in_specs=[VMEM] * (1 + len(got)) + [HBM],
        out_specs=VMEM,
        compiler_params=params(),
        cost_estimate=cost(2),
        name="owned_each",
    )(asked, *got, after)


def gate_kernel(*refs):
    del refs


def gate(*arrays, after=()):
    return pl.pallas_call(
        gate_kernel,
        out_shape=[jax.ShapeDtypeStruct(a.shape, a.dtype) for a in arrays],
        in_specs=[HBM] * (len(arrays) + len(after)),
        out_specs=[HBM] * len(arrays),
        input_output_aliases={i: i for i in range(len(arrays))},
        compiler_params=params(),
        cost_estimate=cost(0),
        name="gate",
    )(*arrays, *after)


def late_kernel(x, *refs):
    out, sem = refs[-2:]
    load_all([pltpu.make_async_copy(x, out, sem)])


def late(x, after):
    return pl.pallas_call(
        late_kernel,
        out_shape=jax.ShapeDtypeStruct(x.shape, x.dtype),
        in_specs=[HBM] * (1 + len(after)),
        out_specs=HBM,
        scratch_shapes=[pltpu.SemaphoreType.DMA(())],
        compiler_params=params(),
        cost_estimate=cost(0),
        name="late",
    )(x, *after)


def ring(x, n):
    return lax.ppermute(x, "tsp", [(i, (i + 1) % n) for i in range(n)])


def flip(x, n, by):
    return lax.ppermute(x, "dp", [(i, i ^ by) for i in range(n)])


def on_device(
    tokens,
    cotangent,
    frozen_key_weight,
    adapter_down_weight,
    adapter_up_weight,
    adapter_place_table,
    segment_adapter,
    segment_live_count,
):
    n_dp = lax.axis_size("dp")
    n = lax.axis_size("tsp")
    me = lax.axis_index("dp").astype(jnp.int32)
    z = lax.axis_index("tsp").astype(jnp.int32)[None]
    held = adapter_down_weight.shape[0]
    segs = segment_adapter.shape[0]
    rows = tokens.shape[0] // segs
    full = segs * rows
    cube = n_dp == 8 and held == 2

    peers = jnp.arange(n_dp, dtype=jnp.int32)
    count = segment_live_count
    ups, downs = adapter_up_weight, adapter_down_weight

    cots = [cotangent, ring(cotangent, n)]
    owner, idx, wanted = plan(me[None], adapter_place_table, segment_adapter, held, n_dp, cube)
    weight = frozen_key_weight.T
    if cube:
        over_x, over_y, weight = gate(flip(downs, n_dp, 2), flip(downs, n_dp, 4), weight)
        ups = late(ups, [over_x, over_y])
    line = [lax.ppermute(ups, "tsp", [(i, (i + s) % n) for i in range(n)]) for s in range(1, n)]
    if cube:
        cots[1], ups, over_x, over_y, *line = gate(cots[1], ups, over_x, over_y, *line)
        corner = [flip(over_x[:1], n_dp, 4), flip(over_y[1:], n_dp, 2)]
    else:
        cots[1], ups, *line = gate(cots[1], ups, *line)

    while len(cots) < n - 1:
        cots.append(ring(cots[-1], n))
    ranks = ups.shape[1]
    size = held * ranks
    info = jnp.zeros((16, ups.shape[2]), ups.dtype).at[0, :n_dp].set(wanted.astype(ups.dtype))
    up_line = jnp.concatenate([u.reshape(size, -1) for u in [ups, *line]] + [info])
    if cube:
        same = [downs, over_x, over_y]
        downs_here = [m for d in same for m in (d, flip(d, n_dp, 1))]
        downs_here += corner + [flip(m, n_dp, 1) for m in corner]
    else:
        downs_here = [lax.all_gather(downs, "dp", axis=0, tiled=True)]
    lowered = project(z, idx, count, tokens, downs_here, n, 4, 4)
    cots[-1], up_line = gate(cots[-1], up_line, after=[lowered[0]])

    cots.append(ring(cots[-1], n))
    if cube:
        same = [up_line] + [flip(up_line, n_dp, k) for k in (2, 4, 6)]
        all_ups = [m for u in same for m in (u, flip(u, n_dp, 1))]
        origin = me[None]
    else:
        all_ups = [lax.all_gather(up_line, "dp", axis=0, tiled=False)[k] for k in range(n_dp)]
        origin = jnp.zeros((1,), jnp.int32)
    asked = told(me[None], all_ups, n * size)
    part = pulled_part(idx, all_ups, cots[:-1], ranks, size, 4, 5)
    cots[-1], *lowered = gate(cots[-1], *lowered, after=[part, asked])

    shift = lambda x, s: lax.ppermute(x, "tsp", [(i, (i + s) % n) for i in range(n)]) if s else x
    parts = [shift(block, s) for s, block in enumerate(lowered)]
    sent, pulled = down_sums(idx, owner, count, tokens, part, cots[-1], all_ups, size, n_dp, n, 4, 7)
    sent, *parts = gate(sent, *parts)
    down_got = lax.all_to_all(sent, "dp", 0, 0, tiled=True)
    lowered = functools.reduce(jnp.add, parts).astype(jnp.bfloat16)
    lowered = [shift(lowered, s) for s in range(n)]
    token_gradient = token_gradients(
        z, idx, count, weight, pulled, downs_here, cots, n, rows, 4, after=lowered[:1]
    )
    lowered[0] = gate(lowered[0], after=[token_gradient])[0]
    got = up_sums(z, origin, owner, cotangent, lowered, n_dp, 2)
    if cube:
        got = [flip(term, n_dp, k) if k else term for k, term in enumerate(got)]
    else:
        got = lax.all_to_all(jnp.stack(got), "dp", 0, 0, tiled=True)
        got = [got[k] for k in range(n_dp)]
    down_grad = owned(origin, asked, down_got, held, 16)
    return token_gradient, down_grad, owned_each(asked, got, held, down_grad)


def solution(mesh):
    placed = (
        P("dp", "tsp"),
        P("dp", "tsp"),
        P("tsp", None),
        P("dp", None, "tsp"),
        P("dp", None, "tsp"),
        P(),
        P("dp"),
        P("dp"),
    )
    return jax.shard_map(
        on_device,
        mesh=mesh,
        in_specs=placed,
        out_specs=(P("dp", "tsp"), P("dp", None, "tsp"), P("dp", None, "tsp")),
        check_vma=False,
    )
```
